32 devices in a mesh: row: 16 (over z, x, core), col: 2 (over y).
Axes of the slice: x: 2, y: 2, z: 4, core: 2. Of those that a mesh axis runs over, the one named last changes fastest.
Arguments:
- rhs: float32 [1015808], P(('row', 'col')), may hold values from -6 to 6
- blocks: float32 [16, 2, 64, 128, 128], P('row', 'col'), may hold values from -0.5 to 0.5
- blk_row: int32 [16, 2, 64], P('row', 'col'), may hold values from 0 to 495
- blk_col: int32 [16, 2, 64], P('row', 'col'), may hold values from 0 to 511
Outputs:
- solution: float32 [131072], P(('col', 'row'))
- rel_residual: float32 [], replicated
The draws below stay inside these ranges and needn't reach their ends.
Inputs may be any that keep to these rules, and one draw needn't show every extreme that they name: `blk_row`: each device holds 64 blocks; blocks listed twice at the same place are added.
All inputs are finite; a program needn't handle non-finite values.
Results may differ from the reference program's by a relative error of at most 0.00013.
Values sent between devices are 32-bit elements; how exact they have to be, the bound alone decides.
No kernel may reach another device: no remote copies, remote signals or barrier semaphores. Data moves between devices by JAX's collectives and lax.ppermute only.
A program may use at most 64 MiB of HBM per device.

```python
import jax
import jax.numpy as jnp
from jax import lax

BLK = 128
ROWB_DEV = 496
COLB_DEV = 512
NB_DEV = 64
ITERS = 3
ROWS = 1015808
N_ROW = 16
N_COL = 2


def set_ends(entries, key, low, top_value):
    dims = entries.shape
    place = [jax.random.randint(jax.random.fold_in(key, axis), (), 0, dims[axis]) for axis in range(len(dims))]
    entries = entries.at[tuple(place)].set(low)
    longest = dims.index(max(dims))
    place[longest] = (place[longest] + 1) % dims[longest]
    return entries.at[tuple(place)].set(top_value)


def block_scale(stream_key, dims, cuts, least, high):
    factor_of = 1.0
    for dim, blocks in cuts:
        steps = jax.random.uniform(jax.random.fold_in(jax.random.fold_in(stream_key, 6), dim), (blocks,), jnp.float32, least / len(cuts), high / len(cuts))
        factor_of = factor_of * jnp.repeat(jnp.exp(steps), dims[dim] // blocks).reshape((-1,) + (1,) * (len(dims) - 1 - dim))
    return factor_of


def scatter_about(stream_key, dims, width, limit, pieces=(), held_as=jnp.bfloat16):
    array = jax.random.normal(stream_key, dims, jnp.float32) * width
    if len(pieces) > 0:
        array = block_scale(stream_key, dims, pieces, -0.22, 0.18) * array
    return jnp.clip(array, min=-limit, max=limit).astype(held_as)


def setup_inputs(seed: int = 0) -> dict:
    keys = jax.random.split(jax.random.key(seed), 5)
    return {
        "rhs": scatter_about(keys[0], (ROWS,), 1.0, 6.0, ((0, 32),), jnp.float32),
        "blocks": scatter_about(keys[1], (N_ROW, N_COL, NB_DEV, BLK, BLK), BLK ** -0.5, 0.5, ((0, 16), (1, 2)), jnp.float32),
        "blk_row": set_ends(jax.random.randint(keys[2], (N_ROW, N_COL, NB_DEV), 0, ROWB_DEV), jax.random.fold_in(keys[2], 1), 0, ROWB_DEV - 1).astype(jnp.int32),
        "blk_col": set_ends(jax.random.randint(keys[3], (N_ROW, N_COL, NB_DEV), 0, COLB_DEV), jax.random.fold_in(keys[3], 1), 0, COLB_DEV - 1).astype(jnp.int32),
    }


def forward(blocks, blk_row, blk_col, vec):
    parts = vec.reshape(N_COL, COLB_DEV, BLK)
    col_index = jnp.arange(N_COL, dtype=jnp.int32)[None, :, None]
    picked = parts[col_index, blk_col]
    prod = jnp.einsum('rcnij,rcnj->rcni', blocks, picked, precision=lax.Precision.HIGHEST)
    rows = jnp.arange(N_ROW, dtype=jnp.int32)[:, None, None] * ROWB_DEV + blk_row
    total = jnp.zeros((N_ROW * ROWB_DEV, BLK), jnp.float32).at[rows].add(prod)
    return total.reshape(N_ROW * ROWB_DEV * BLK)

def backward(blocks, blk_row, blk_col, vec):
    parts = vec.reshape(N_ROW, ROWB_DEV, BLK)
    row_index = jnp.arange(N_ROW, dtype=jnp.int32)[:, None, None]
    picked = parts[row_index, blk_row]
    prod = jnp.einsum('rcnij,rcni->rcnj', blocks, picked, precision=lax.Precision.HIGHEST)
    cols = jnp.arange(N_COL, dtype=jnp.int32)[None, :, None] * COLB_DEV + blk_col
    total = jnp.zeros((N_COL * COLB_DEV, BLK), jnp.float32).at[cols].add(prod)
    return total.reshape(N_COL * COLB_DEV * BLK)

def reference(rhs, blocks, blk_row, blk_col):
    beta_first = jnp.sqrt(jnp.sum(rhs * rhs))
    u = rhs / beta_first
    v_raw = backward(blocks, blk_row, blk_col, u)
    alpha = jnp.sqrt(jnp.sum(v_raw * v_raw))
    v = v_raw / alpha
    w = v
    solution = jnp.zeros_like(v)
    phibar = beta_first
    rhobar = alpha
    for step in range(ITERS):
        u_raw = forward(blocks, blk_row, blk_col, v) - alpha * u
        beta = jnp.sqrt(jnp.sum(u_raw * u_raw))
        u = u_raw / beta
        v_raw = backward(blocks, blk_row, blk_col, u) - beta * v
        alpha = jnp.sqrt(jnp.sum(v_raw * v_raw))
        v = v_raw / alpha
        rho = jnp.sqrt(rhobar * rhobar + beta * beta)
        cosine = rhobar / rho
        sine = beta / rho
        theta = sine * alpha
        rhobar = -cosine * alpha
        phi = cosine * phibar
        phibar = sine * phibar
        solution = solution + phi / rho * w
        w = v - theta / rho * w
    return (solution, phibar / beta_first)
```

```python
import functools

import jax
import jax.numpy as jnp
from jax import lax
from jax.experimental import pallas as pl
from jax.experimental.pallas import tpu as pltpu
from jax.sharding import PartitionSpec as P

BLK = 128
ROWB_DEV = 496
COLB_DEV = 512
NB_DEV = 64
ITERS = 3
MSG = NB_DEV + 8
VMEM_LIMIT = 24 * 1024 * 1024

f32 = jnp.float32
bf16 = jnp.bfloat16


def total(x):
    s = jnp.sum(jnp.sum(x, axis=0, keepdims=True), axis=1, keepdims=True)
    return jnp.broadcast_to(s, (1, BLK))


def place_sum(index_row, parts, rows):
    k = parts.shape[0]
    at = lax.broadcasted_iota(jnp.int32, (rows, k), 0).astype(f32)
    hot = jnp.where(at == index_row, 1.0, 0.0).astype(bf16)
    high = parts.astype(bf16)
    rest = parts - high.astype(f32)
    mid = rest.astype(bf16)
    low = (rest - mid.astype(f32)).astype(bf16)
    three = jnp.concatenate([high, mid, low], axis=1)
    out = jnp.dot(hot, three, preferred_element_type=f32)
    return out[:, :BLK] + (out[:, BLK : 2 * BLK] + out[:, 2 * BLK :])


def write_message(msg, index_row, square):
    msg[NB_DEV : NB_DEV + 1, :] = index_row
    msg[NB_DEV + 1 : NB_DEV + 2, :] = square
    msg[NB_DEV + 2 :, :] = jnp.zeros((MSG - NB_DEV - 2, BLK), f32)


def times_blocks_t(blocks, picked, msg):
    cols = picked[...].T
    for n in range(NB_DEV):
        prod = blocks[n * BLK : (n + 1) * BLK, :] * cols[:, n : n + 1]
        msg[n : n + 1, :] = jnp.sum(prod, axis=0, keepdims=True)


def times_blocks(blocks, at, vec, msg):
    lane = lax.broadcasted_iota(jnp.int32, (BLK, BLK), 1)
    acc = jnp.zeros((BLK, BLK), f32)
    for n in range(NB_DEV):
        prod = blocks[n * BLK : (n + 1) * BLK, :] * vec[pl.ds(at[n], 1), :]
        acc = jnp.where(lane == n, jnp.sum(prod, axis=1, keepdims=True), acc)
    msg[:NB_DEV, :] = acc.T[:NB_DEV, :]


def first_kernel(rows_at, u_raw, blocks, col_row, msg, picked):
    for n in range(NB_DEV):
        picked[n : n + 1, :] = u_raw[pl.ds(rows_at[n], 1), :]
    u = u_raw[...]
    times_blocks_t(blocks, picked, msg)
    write_message(msg, col_row[...], total(u * u))


def gather_sum_kernel(slot, is_first, own, *refs):
    *others, out = refs
    first = is_first[0] > 0
    lane = lax.broadcasted_iota(jnp.int32, (1, BLK), 1)
    parts, index, square = [], [], jnp.zeros((1, BLK), f32)
    for k, other in enumerate(others):
        m = jnp.where(first, own[...], other[...]) if k == slot else other[...]
        a, b = m[:MSG], m[MSG:]
        parts += [a[:NB_DEV], b[:NB_DEV]]
        index.append(jnp.where(lane < NB_DEV, a[NB_DEV : NB_DEV + 1], b[NB_DEV : NB_DEV + 1]))
        square = square + (a[NB_DEV + 1 : NB_DEV + 2] + b[NB_DEV + 1 : NB_DEV + 2])
    out[:COLB_DEV, :] = place_sum(jnp.concatenate(index, axis=1), jnp.concatenate(parts, axis=0), COLB_DEV)
    out[COLB_DEV:, :] = jnp.broadcast_to(square, (8, BLK))


def v_kernel(has_before, cols_at, half, other, *refs):
    if has_before:
        v_raw_before, alpha, blocks, v_raw, msg, beta_out = refs
    else:
        blocks, v_raw, msg, beta_out = refs
    beta = jnp.sqrt(half[COLB_DEV : COLB_DEV + 1, :] + other[COLB_DEV : COLB_DEV + 1, :])
    v = (half[:COLB_DEV, :] + other[:COLB_DEV, :]) / beta
    if has_before:
        v = v - v_raw_before[...] * (beta / alpha[:1, :])
    v_raw[...] = v
    beta_out[...] = jnp.broadcast_to(beta, (8, BLK))
    write_message(msg, jnp.zeros((1, BLK), f32), total(v * v))
    times_blocks(blocks, cols_at, v_raw, msg)


def u_kernel(n_col, last, rows_at, row_index, u_raw_before, beta, *refs):
    pieces, refs = refs[:n_col], refs[n_col:]
    if last:
        square_out, alpha_out = refs
    else:
        blocks, col_row, u_raw, msg, alpha_out, picked = refs
    square = pieces[0][NB_DEV + 1 : NB_DEV + 2, :]
    for piece in pieces[1:]:
        square = square + piece[NB_DEV + 1 : NB_DEV + 2, :]
    alpha = jnp.sqrt(square)
    alpha_out[...] = jnp.broadcast_to(alpha, (8, BLK))
    prods = jnp.concatenate([piece[:NB_DEV, :] for piece in pieces], axis=0)
    front = place_sum(row_index[...], prods, ROWB_DEV)
    u = front / alpha - u_raw_before[...] * (alpha / beta[:1, :])
    square = total(u * u)
    if last:
        square_out[...] = jnp.broadcast_to(square, (8, BLK))
        return
    u_raw[...] = u
    for n in range(NB_DEV):
        picked[n : n + 1, :] = u_raw[pl.ds(rows_at[n], 1), :]
    times_blocks_t(blocks, picked, msg)
    write_message(msg, col_row[...], square)


def end_kernel(square, *refs):
    v_raws, alphas, betas = refs[:ITERS], refs[ITERS : 2 * ITERS], refs[2 * ITERS : 3 * ITERS]
    out, residual = refs[3 * ITERS :]
    alpha = [a[:1, :] for a in alphas]
    beta = [b[:1, :] for b in betas] + [jnp.sqrt(square[:1, :])]
    phibar, rhobar = beta[0], alpha[0]
    x = None
    for k in range(ITERS):
        v = v_raws[k][...] / alpha[k]
        w = v if k == 0 else v - turn * w
        rho = jnp.sqrt(rhobar * rhobar + beta[k + 1] * beta[k + 1])
        cosine, sine = rhobar / rho, beta[k + 1] / rho
        phi = cosine * phibar
        phibar = sine * phibar
        step = phi / rho * w
        x = step if x is None else x + step
        if k + 1 < ITERS:
            turn = sine * alpha[k + 1] / rho
            rhobar = -cosine * alpha[k + 1]
    out[...] = x
    residual[...] = jnp.broadcast_to(phibar / beta[0], (8, BLK))


def call(body, ins, outs, smem=0, scratch=()):
    specs = [pl.BlockSpec(memory_space=pltpu.SMEM)] * smem
    specs += [pl.BlockSpec(memory_space=pltpu.VMEM)] * (len(ins) - smem)
    return pl.pallas_call(
        body,
        out_shape=[jax.ShapeDtypeStruct(s, f32) for s in outs],
        in_specs=specs,
        out_specs=[pl.BlockSpec(memory_space=pltpu.VMEM)] * len(outs),
        scratch_shapes=list(scratch),
        compiler_params=pltpu.CompilerParams(vmem_limit_bytes=VMEM_LIMIT),
    )(*ins)


def chip_steps(chips):
    if chips == 8:
        return [(1, 4), (3, 3), (2, 6), (5, 7)], 1
    steps = [(m, m + 1) for m in range(1, chips - 1, 2)] + [(chips - 1, chips - 1)]
    return steps, len(steps) - 1


def on_device(n_row, n_col, rhs, blocks, blk_row, blk_col):
    chips = n_row // 2
    steps, twice = chip_steps(chips)
    per_rhs = rhs.shape[0] // BLK
    per_out = COLB_DEV // n_row
    row, col = lax.axis_index("row"), lax.axis_index("col")
    is_first = (row % 2 == 0).astype(jnp.int32).reshape(1)

    def swap(x):
        return lax.ppermute(x, "row", [(r, r ^ 1) for r in range(n_row)])

    def to_chips(x):
        return [
            lax.ppermute(x, "row", [(r, r ^ (2 * step[r % 2])) for r in range(n_row)]) for step in steps
        ]

    def around_col(x):
        return [x] + [
            lax.ppermute(x, "col", [(i, (i - s) % n_col) for i in range(n_col)]) for s in range(1, n_col)
        ]

    tiles = blocks.reshape(NB_DEV * BLK, BLK)
    cols_at = blk_col.reshape(NB_DEV)
    rows_here = blk_row.reshape(NB_DEV)
    col_row = jnp.concatenate([cols_at, cols_at]).astype(f32).reshape(1, BLK)
    row_row = jnp.concatenate([rows_here, rows_here]).astype(f32).reshape(1, BLK)

    first = jnp.concatenate([rhs.reshape(per_rhs, BLK), jnp.broadcast_to(row_row, (8, BLK))])
    got = around_col(first)
    u_raw = jnp.concatenate([g[:per_rhs] for g in got])
    index = jnp.concatenate([g[per_rhs, :NB_DEV] for g in got]).astype(jnp.int32)
    row_index = jnp.remainder(index - col * per_rhs, ROWB_DEV).astype(f32).reshape(1, n_col * NB_DEV)
    rows_at = jnp.remainder(rows_here - col * per_rhs, ROWB_DEV)

    picked = [pltpu.VMEM((NB_DEV, BLK), f32)]

    def gather(msg):
        both = jnp.concatenate([msg, swap(msg)])
        others = to_chips(both)
        (half,) = call(
            functools.partial(gather_sum_kernel, twice), [is_first, both] + others, [(COLB_DEV + 8, BLK)], smem=1
        )
        return half, swap(half)

    (msg,) = call(first_kernel, [rows_at, u_raw, tiles, col_row], [(MSG, BLK)], smem=1, scratch=picked)
    alphas, betas, v_raws = [], [], []
    for step in range(ITERS):
        half, other = gather(msg)
        before = [v_raws[-1], alphas[-1]] if step else []
        v_raw, msg, beta = call(
            functools.partial(v_kernel, step > 0),
            [cols_at, half, other] + before + [tiles],
            [(COLB_DEV, BLK), (MSG, BLK), (8, BLK)],
            smem=1,
        )
        v_raws.append(v_raw)
        betas.append(beta)
        last = step + 1 == ITERS
        ins = [rows_at, row_index, u_raw, beta] + around_col(msg)
        body = functools.partial(u_kernel, n_col, last)
        if last:
            square, alpha = call(body, ins, [(8, BLK), (8, BLK)], smem=1)
        else:
            u_raw, msg, alpha = call(
                body,
                ins + [tiles, col_row],
                [(ROWB_DEV, BLK), (MSG, BLK), (8, BLK)],
                smem=1,
                scratch=picked,
            )
        alphas.append(alpha)

    both = square + swap(square)
    parts = to_chips(both)
    parts[twice] = jnp.where(is_first[0] > 0, both, parts[twice])
    half = functools.reduce(lambda a, b: a + b, parts)
    square = half + swap(half)
    mine = [lax.dynamic_slice_in_dim(v, row * per_out, per_out) for v in v_raws]
    out, residual = call(end_kernel, [square] + mine + alphas + betas, [(per_out, BLK), (8, BLK)])
    return out.reshape(per_out * BLK), residual[0, 0]


def solution(mesh):
    return jax.shard_map(
        functools.partial(on_device, mesh.shape["row"], mesh.shape["col"]),
        mesh=mesh,
        in_specs=(
            P(("row", "col")),
            P("row", "col", None, None, None),
            P("row", "col", None),
            P("row", "col", None),
        ),
        out_specs=(P(("col", "row")), P()),
        check_vma=False,
    )
```

```python
import functools

import jax
import jax.numpy as jnp
from jax import lax
from jax.experimental import pallas as pl
from jax.experimental.pallas import tpu as pltpu
from jax.sharding import PartitionSpec as P

BLK = 128
ROWB_DEV = 496
COLB_DEV = 512
NB_DEV = 64
ITERS = 3
MSG = NB_DEV + 8
INDEX, SQUARE = NB_DEV, NB_DEV + 1
COL_ROW, ROW_ROW, SHIFT, IS_FIRST = (slice(k, k + 1) for k in range(4))
ROWS_HELD = 512
PARTS = 8
VMEM_LIMIT = 16 * 1024 * 1024

f32 = jnp.float32
bf16 = jnp.bfloat16


def total(x):
    s = jnp.sum(jnp.sum(x, axis=0, keepdims=True), axis=1, keepdims=True)
    return jnp.broadcast_to(s, (1, BLK))


def halves(x):
    high = x.astype(bf16)
    return high, (x - high.astype(f32)).astype(bf16)


def place_sum(index_row, parts, rows):
    k = parts.shape[0]
    at = lax.broadcasted_iota(jnp.int32, (rows, k), 0).astype(f32)
    hot = jnp.where(at == index_row, 1.0, 0.0).astype(bf16)
    high = parts.astype(bf16)
    rest = parts - high.astype(f32)
    mid = rest.astype(bf16)
    low = (rest - mid.astype(f32)).astype(bf16)
    three = jnp.concatenate([high, mid, low], axis=1)
    out = jnp.dot(hot, three, preferred_element_type=f32)
    return out[:, :BLK] + (out[:, BLK : 2 * BLK] + out[:, 2 * BLK :])


def pick(at, x):
    rows = x.shape[0]
    lane = lax.broadcasted_iota(jnp.int32, (NB_DEV, rows), 1).astype(f32)
    hot = jnp.where(lane == jnp.concatenate([at] * (rows // BLK), axis=1), 1.0, 0.0).astype(bf16)
    return jnp.dot(hot, jnp.concatenate(halves(x), axis=1), preferred_element_type=f32)


def times_tiles(tiles, first, picked, msg):
    per = 8
    row = lax.broadcasted_iota(jnp.int32, (2 * per, BLK), 0)
    for g in range(0, NB_DEV, per):
        both = jnp.concatenate([picked[g : g + per, :BLK], picked[g : g + per, BLK:]], axis=0)
        lhs = jnp.concatenate([jnp.where(row % per == t, both, 0.0) for t in range(per)], axis=1).astype(bf16)
        out = jnp.dot(lhs, tiles[(first + g) * BLK : (first + g + per) * BLK, :], preferred_element_type=f32)
        out = out[:, :BLK] + out[:, BLK:]
        msg[g : g + per, :] = out[:per] + out[per:]


def write_end(msg, index_row, square):
    row = lax.broadcasted_iota(jnp.int32, (MSG - NB_DEV, BLK), 0)
    msg[NB_DEV:, :] = jnp.where(row == 0, index_row, jnp.where(row == 1, square, 0.0))


def tiles_kernel(blocks, out, held, sems):
    per = held.shape[0] // PARTS
    parts = [
        pltpu.make_async_copy(blocks.at[pl.ds(k * per, per)], held.at[pl.ds(k * per, per)], sems.at[k])
        for k in range(PARTS)
    ]
    for part in parts:
        part.start()
    for k, part in enumerate(parts):
        part.wait()
        for at in range(k * per, (k + 1) * per, BLK):
            block = held[at : at + BLK, :]
            for where, x in ((at, block), (held.shape[0] + at, block.T)):
                high, low = halves(x)
                out[where : where + BLK, :BLK] = high
                out[where : where + BLK, BLK:] = low


def first_kernel(n_col, tiles, *refs):
    pieces, (consts, ats, u_raw, msg, consts_out, ats_out) = refs[:n_col], refs[n_col:]
    consts_out[...] = consts[...]
    ats_out[...] = ats[...]
    per = pieces[0].shape[0]
    for k, piece in enumerate(pieces):
        u_raw[k * per : (k + 1) * per, :] = piece[...]
    u_raw[ROWB_DEV:, :] = jnp.zeros((ROWS_HELD - ROWB_DEV, BLK), f32)
    u = u_raw[...]
    times_tiles(tiles, 0, pick(ats[:NB_DEV, :], u), msg)
    write_end(msg, consts[COL_ROW, :], total(u * u))


def gather_sum_kernel(slot, tiles, consts, own, *refs):
    *others, out = refs
    first = consts[IS_FIRST, :] > 0
    n = 2 * NB_DEV
    parts, index, square = [], [], jnp.zeros((1, BLK), f32)
    for k, other in enumerate(others):
        m = jnp.where(first, own[...], other[...]) if k == slot else other[...]
        parts.append(m[:n])
        index.append(m[n : n + 1])
        square = square + m[n + 1 : n + 2]
    out[:COLB_DEV, :] = place_sum(jnp.concatenate(index, axis=1), jnp.concatenate(parts, axis=0), COLB_DEV)
    out[COLB_DEV:, :] = jnp.broadcast_to(square, (8, BLK))


def v_kernel(has_before, tiles, half, other, *refs):
    if has_before:
        v_raw_before, alpha, consts, ats, v_raw, msg, beta_out = refs
    else:
        consts, ats, v_raw, msg, beta_out = refs
    beta = jnp.sqrt(half[COLB_DEV : COLB_DEV + 1, :] + other[COLB_DEV : COLB_DEV + 1, :])
    v = (half[:COLB_DEV, :] + other[:COLB_DEV, :]) / beta
    if has_before:
        v = v - v_raw_before[...] * (beta / alpha[:1, :])
    v_raw[...] = v
    beta_out[...] = jnp.broadcast_to(beta, (8, BLK))
    times_tiles(tiles, NB_DEV, pick(ats[NB_DEV:, :], v), msg)
    write_end(msg, consts[ROW_ROW, :], total(v * v))


def u_kernel(n_col, last, *refs):
    if not last:
        tiles, *refs = refs
    consts, u_raw_before, beta, *refs = refs
    pieces, refs = refs[:n_col], refs[n_col:]
    if last:
        square_out, alpha_out = refs
    else:
        ats, u_raw, msg, alpha_out = refs
    square = pieces[0][SQUARE : SQUARE + 1, :]
    for piece in pieces[1:]:
        square = square + piece[SQUARE : SQUARE + 1, :]
    alpha = jnp.sqrt(square)
    alpha_out[...] = jnp.broadcast_to(alpha, (8, BLK))
    lane = lax.broadcasted_iota(jnp.int32, (1, BLK), 1)
    index = [
        jnp.where(lane < NB_DEV, a[INDEX : INDEX + 1, :], b[INDEX : INDEX + 1, :])
        for a, b in zip(pieces[::2], pieces[1::2])
    ]
    index = jnp.concatenate([i - consts[SHIFT, :] for i in index], axis=1)
    index = jnp.where(index < 0, index + ROWB_DEV, index)
    prods = jnp.concatenate([piece[:NB_DEV, :] for piece in pieces], axis=0)
    front = place_sum(index, prods, ROWS_HELD)
    u = front / alpha - u_raw_before[...] * (alpha / beta[:1, :])
    square = total(u * u)
    if last:
        square_out[...] = jnp.broadcast_to(square, (8, BLK))
        return
    u_raw[...] = u
    times_tiles(tiles, 0, pick(ats[:NB_DEV, :], u), msg)
    write_end(msg, consts[COL_ROW, :], square)


def end_kernel(square, *refs):
    v_raws, alphas, betas = refs[:ITERS], refs[ITERS : 2 * ITERS], refs[2 * ITERS : 3 * ITERS]
    out, residual = refs[3 * ITERS :]
    alpha = [a[:1, :] for a in alphas]
    beta = [b[:1, :] for b in betas] + [jnp.sqrt(square[:1, :])]
    phibar, rhobar = beta[0], alpha[0]
    x = None
    for k in range(ITERS):
        v = v_raws[k][...] / alpha[k]
        w = v if k == 0 else v - turn * w
        rho = jnp.sqrt(rhobar * rhobar + beta[k + 1] * beta[k + 1])
        cosine, sine = rhobar / rho, beta[k + 1] / rho
        phi = cosine * phibar
        phibar = sine * phibar
        step = phi / rho * w
        x = step if x is None else x + step
        if k + 1 < ITERS:
            turn = sine * alpha[k + 1] / rho
            rhobar = -cosine * alpha[k + 1]
    out[...] = x
    residual[...] = (phibar / beta[0])[:, :1]


def split_tiles(blocks):
    rows = blocks.shape[0]
    return pl.pallas_call(
        tiles_kernel,
        out_shape=pltpu.VMEM((2 * rows, 2 * BLK), bf16),
        in_specs=[pl.BlockSpec(memory_space=pl.ANY)],
        out_specs=pl.BlockSpec(memory_space=pltpu.VMEM),
        scratch_shapes=[pltpu.VMEM((rows, BLK), f32), pltpu.SemaphoreType.DMA((PARTS,))],
        compiler_params=pltpu.CompilerParams(vmem_limit_bytes=VMEM_LIMIT),
        cost_estimate=pl.CostEstimate(flops=0, bytes_accessed=4 * rows * BLK, transcendentals=0),
    )(pltpu.with_memory_space_constraint(blocks, pltpu.HBM))


def call(body, tiles, ins, outs):
    if tiles is not None:
        ins = [pltpu.with_memory_space_constraint(tiles, pltpu.VMEM)] + ins
    return pl.pallas_call(
        body,
        out_shape=[jax.ShapeDtypeStruct(s, f32) for s in outs],
        in_specs=[pl.BlockSpec(memory_space=pltpu.VMEM)] * len(ins),
        out_specs=[pl.BlockSpec(memory_space=pltpu.VMEM)] * len(outs),
        compiler_params=pltpu.CompilerParams(vmem_limit_bytes=VMEM_LIMIT),
    )(*ins)


def chip_steps(chips):
    if chips == 8:
        return [(1, 4), (3, 3), (2, 6), (5, 7)], 1
    steps = [(m, m + 1) for m in range(1, chips - 1, 2)] + [(chips - 1, chips - 1)]
    return steps, len(steps) - 1


def on_device(n_row, n_col, rhs, blocks, blk_row, blk_col):
    chips = n_row // 2
    steps, twice = chip_steps(chips)
    per_rhs = rhs.shape[0] // BLK
    per_out = COLB_DEV // n_row
    row, col = lax.axis_index("row"), lax.axis_index("col")

    def swap(x):
        return lax.ppermute(x, "row", [(r, r ^ 1) for r in range(n_row)])

    def to_chips(x):
        return [
            lax.ppermute(x, "row", [(r, r ^ (2 * step[r % 2])) for r in range(n_row)]) for step in steps
        ]

    def around_col(x):
        return [x] + [
            lax.ppermute(x, "col", [(i, (i - s) % n_col) for i in range(n_col)]) for s in range(1, n_col)
        ]

    pieces = around_col(rhs.reshape(per_rhs, BLK))
    shift = col * per_rhs

    blocks = blocks.reshape(NB_DEV * BLK, BLK)
    tiles = split_tiles(blocks)
    cols_here = blk_col.reshape(NB_DEV)
    rows_here = blk_row.reshape(NB_DEV)
    rows_turned = jnp.where(rows_here < shift, rows_here - shift + ROWB_DEV, rows_here - shift)
    consts = jnp.stack(
        [
            jnp.concatenate([cols_here, cols_here]),
            jnp.concatenate([rows_here, rows_here]),
            jnp.full((BLK,), shift),
            jnp.full((BLK,), 1 - row % 2),
        ]
        + [jnp.zeros((BLK,), jnp.int32)] * 4
    ).astype(f32)
    ats = jnp.concatenate([rows_turned, cols_here]).astype(f32)
    ats = jnp.broadcast_to(ats[:, None], (2 * NB_DEV, BLK))
    lane = lax.broadcasted_iota(jnp.int32, (MSG - NB_DEV, BLK), 1)
    end_row = lax.broadcasted_iota(jnp.int32, (MSG - NB_DEV, BLK), 0)

    def gather(msg):
        peer = swap(msg)
        a, b = msg[NB_DEV:], peer[NB_DEV:]
        end = jnp.where(end_row == 0, jnp.where(lane < NB_DEV, a, b), a + b)
        both = jnp.concatenate([msg[:NB_DEV], peer[:NB_DEV], end])
        others = to_chips(both)
        (half,) = call(
            functools.partial(gather_sum_kernel, twice), tiles, [consts, both] + others, [(COLB_DEV + 8, BLK)]
        )
        return half, swap(half)

    u_raw, msg, consts, ats = call(
        functools.partial(first_kernel, n_col),
        tiles,
        pieces + [consts, ats],
        [(ROWS_HELD, BLK), (MSG, BLK), consts.shape, ats.shape],
    )
    alphas, betas, v_raws = [], [], []
    for step in range(ITERS):
        half, other = gather(msg)
        before = [v_raws[-1], alphas[-1]] if step else []
        v_raw, msg, beta = call(
            functools.partial(v_kernel, step > 0),
            tiles,
            [half, other] + before + [consts, ats],
            [(COLB_DEV, BLK), (MSG, BLK), (8, BLK)],
        )
        v_raws.append(v_raw)
        betas.append(beta)
        last = step + 1 == ITERS
        ins = [consts, u_raw, beta] + around_col(msg)
        body = functools.partial(u_kernel, n_col, last)
        if last:
            square, alpha = call(body, None, ins, [(8, BLK), (8, BLK)])
        else:
            u_raw, msg, alpha = call(
                body, tiles, ins + [ats], [(ROWS_HELD, BLK), (MSG, BLK), (8, BLK)]
            )
        alphas.append(alpha)

    both = square + swap(square)
    parts = to_chips(both)
    parts[twice] = jnp.where(row % 2 == 0, both, parts[twice])
    half = functools.reduce(lambda a, b: a + b, parts)
    square = half + swap(half)
    mine = [lax.dynamic_slice_in_dim(v, row * per_out, per_out) for v in v_raws]
    out, residual = call(end_kernel, None, [square] + mine + alphas + betas, [(per_out, BLK), (1, 1)])
    return out.reshape(per_out * BLK), residual.reshape(())


def solution(mesh):
    return jax.shard_map(
        functools.partial(on_device, mesh.shape["row"], mesh.shape["col"]),
        mesh=mesh,
        in_specs=(
            P(("row", "col")),
            P("row", "col", None, None, None),
            P("row", "col", None),
            P("row", "col", None),
        ),
        out_specs=(P(("col", "row")), P()),
        check_vma=False,
    )
```

```python
import functools

import jax
import jax.numpy as jnp
from jax import lax
from jax.experimental import pallas as pl
from jax.experimental.pallas import tpu as pltpu
from jax.sharding import PartitionSpec as P

BLK = 128
ROWB_DEV = 496
COLB_DEV = 512
NB_DEV = 64
ITERS = 3
MSG = NB_DEV + 8
INDEX, SQUARE = NB_DEV, NB_DEV + 1
COL_ROW, ROW_ROW, SHIFT = (slice(k, k + 1) for k in range(3))
ROWS_HELD = 512
PARTS = 8
VMEM_LIMIT = 16 * 1024 * 1024

f32 = jnp.float32
bf16 = jnp.bfloat16


def total(x):
    s = jnp.sum(jnp.sum(x, axis=0, keepdims=True), axis=1, keepdims=True)
    return jnp.broadcast_to(s, (1, BLK))


def halves(x):
    high = x.astype(bf16)
    return high, (x - high.astype(f32)).astype(bf16)


def place_sum(index_row, parts, rows):
    k = parts.shape[0]
    at = lax.broadcasted_iota(jnp.int32, (rows, k), 0).astype(f32)
    hot = jnp.where(at == index_row, 1.0, 0.0).astype(bf16)
    out = jnp.dot(hot, jnp.concatenate(halves(parts), axis=1), preferred_element_type=f32)
    return out[:, :BLK] + out[:, BLK:]


def pick(at, x):
    rows = x.shape[0]
    lane = lax.broadcasted_iota(jnp.int32, (NB_DEV, rows), 1).astype(f32)
    hot = jnp.where(lane == jnp.concatenate([at] * (rows // BLK), axis=1), 1.0, 0.0).astype(bf16)
    return jnp.dot(hot, jnp.concatenate(halves(x), axis=1), preferred_element_type=f32)


def times_tiles(tiles, first, picked, msg):
    per = 8
    row = lax.broadcasted_iota(jnp.int32, (2 * per, BLK), 0)
    for g in range(0, NB_DEV, per):
        both = jnp.concatenate([picked[g : g + per, :BLK], picked[g : g + per, BLK:]], axis=0)
        lhs = jnp.concatenate([jnp.where(row % per == t, both, 0.0) for t in range(per)], axis=1).astype(bf16)
        out = jnp.dot(lhs, tiles[(first + g) * BLK : (first + g + per) * BLK, :], preferred_element_type=f32)
        out = out[:, :BLK] + out[:, BLK:]
        msg[g : g + per, :] = out[:per] + out[per:]


def write_end(msg, index_row, square):
    row = lax.broadcasted_iota(jnp.int32, (MSG - NB_DEV, BLK), 0)
    msg[NB_DEV:, :] = jnp.where(row == 0, index_row, jnp.where(row == 1, square, 0.0))


def tiles_kernel(blocks, blk_row, blk_col, rhs, place, out, consts, ats, mine, held, rows_held, cols_held, sems):
    per = held.shape[0] // PARTS
    few = [
        pltpu.make_async_copy(a, b, sems.at[PARTS + k])
        for k, (a, b) in enumerate(((blk_row, rows_held), (blk_col, cols_held), (rhs, mine)))
    ]
    parts = [
        pltpu.make_async_copy(blocks.at[pl.ds(k * per, per)], held.at[pl.ds(k * per, per)], sems.at[k])
        for k in range(PARTS)
    ]
    for part in few + parts:
        part.start()
    for part in few:
        part.wait()
    rows, cols = rows_held[...].astype(f32), cols_held[...].astype(f32)
    shift = place[:1, :]
    consts[COL_ROW, :] = jnp.concatenate([cols, cols], axis=1)
    consts[ROW_ROW, :] = jnp.concatenate([rows, rows], axis=1)
    consts[SHIFT, :] = shift
    consts[3:, :] = jnp.zeros((5, BLK), f32)
    turned = rows - shift[:, :NB_DEV]
    turned = jnp.where(turned < 0, turned + ROWB_DEV, turned)
    ats[...] = jnp.broadcast_to(jnp.concatenate([turned, cols], axis=1), (2 * NB_DEV, BLK)).T
    for k, part in enumerate(parts):
        part.wait()
        for at in range(k * per, (k + 1) * per, BLK):
            for lane, half in zip((0, BLK), halves(held[at : at + BLK, :])):
                out[at : at + BLK, lane : lane + BLK] = half
                out[held.shape[0] + at : held.shape[0] + at + BLK, lane : lane + BLK] = half.T


def first_kernel(n_col, tiles, *refs):
    pieces, (consts, ats, u_raw, msg) = refs[:n_col], refs[n_col:]
    per = pieces[0].shape[0]
    for k, piece in enumerate(pieces):
        u_raw[k * per : (k + 1) * per, :] = piece[...]
    u_raw[ROWB_DEV:, :] = jnp.zeros((ROWS_HELD - ROWB_DEV, BLK), f32)
    u = u_raw[...]
    times_tiles(tiles, 0, pick(ats[:NB_DEV, :], u), msg)
    write_end(msg, consts[COL_ROW, :], total(u * u))


def gather_sum_kernel(tiles, own, near, *refs):
    *chips, out = refs
    lane = lax.broadcasted_iota(jnp.int32, (1, BLK), 1)
    parts = [own[:NB_DEV], near[:NB_DEV]]
    index = [jnp.where(lane < NB_DEV, own[INDEX : INDEX + 1], near[INDEX : INDEX + 1])]
    square = own[SQUARE : SQUARE + 1] + near[SQUARE : SQUARE + 1]
    n = 2 * NB_DEV
    for chip in chips:
        parts.append(chip[:n])
        index.append(chip[n : n + 1])
        square = square + chip[n + 1 : n + 2]
    out[:COLB_DEV, :] = place_sum(jnp.concatenate(index, axis=1), jnp.concatenate(parts, axis=0), COLB_DEV)
    out[COLB_DEV:, :] = jnp.broadcast_to(square, (8, BLK))


def v_kernel(has_before, tiles, half, other, *refs):
    if has_before:
        v_raw_before, alpha, consts, ats, v_raw, msg, beta_out = refs
    else:
        consts, ats, v_raw, msg, beta_out = refs
    beta = jnp.sqrt(half[COLB_DEV : COLB_DEV + 1, :] + other[COLB_DEV : COLB_DEV + 1, :])
    v = (half[:COLB_DEV, :] + other[:COLB_DEV, :]) / beta
    if has_before:
        v = v - v_raw_before[...] * (beta / alpha[:1, :])
    v_raw[...] = v
    beta_out[...] = jnp.broadcast_to(beta, (8, BLK))
    times_tiles(tiles, NB_DEV, pick(ats[NB_DEV:, :], v), msg)
    write_end(msg, consts[ROW_ROW, :], total(v * v))


def u_kernel(n_col, last, *refs):
    if not last:
        tiles, *refs = refs
    consts, u_raw_before, beta, *refs = refs
    pieces, refs = refs[:n_col], refs[n_col:]
    if last:
        square_out, alpha_out = refs
    else:
        ats, u_raw, msg, alpha_out = refs
    square = pieces[0][SQUARE : SQUARE + 1, :]
    for piece in pieces[1:]:
        square = square + piece[SQUARE : SQUARE + 1, :]
    alpha = jnp.sqrt(square)
    alpha_out[...] = jnp.broadcast_to(alpha, (8, BLK))
    lane = lax.broadcasted_iota(jnp.int32, (1, BLK), 1)
    index = [
        jnp.where(lane < NB_DEV, a[INDEX : INDEX + 1, :], b[INDEX : INDEX + 1, :])
        for a, b in zip(pieces[::2], pieces[1::2])
    ]
    index = jnp.concatenate([i - consts[SHIFT, :] for i in index], axis=1)
    index = jnp.where(index < 0, index + ROWB_DEV, index)
    prods = jnp.concatenate([piece[:NB_DEV, :] for piece in pieces], axis=0)
    front = place_sum(index, prods, ROWS_HELD)
    u = front / alpha - u_raw_before[...] * (alpha / beta[:1, :])
    square = total(u * u)
    if last:
        square_out[...] = jnp.broadcast_to(square, (8, BLK))
        return
    u_raw[...] = u
    times_tiles(tiles, 0, pick(ats[:NB_DEV, :], u), msg)
    write_end(msg, consts[COL_ROW, :], square)


def before_end_kernel(*refs):
    v_raws, alphas, betas = refs[:ITERS], refs[ITERS : 2 * ITERS], refs[2 * ITERS : 3 * ITERS]
    x_out, w_out, scalars = refs[3 * ITERS :]
    alpha = [a[:1, :] for a in alphas]
    beta = [b[:1, :] for b in betas]
    phibar, rhobar = beta[0], alpha[0]
    x = jnp.zeros(x_out.shape, f32)
    w = v_raws[0][...] / alpha[0]
    for k in range(1, ITERS):
        rho = jnp.sqrt(rhobar * rhobar + beta[k] * beta[k])
        cosine, sine = rhobar / rho, beta[k] / rho
        phi = cosine * phibar
        phibar = sine * phibar
        x = x + phi / rho * w
        w = v_raws[k][...] / alpha[k] - sine * alpha[k] / rho * w
        rhobar = -cosine * alpha[k]
    x_out[...] = x
    w_out[...] = w
    row = lax.broadcasted_iota(jnp.int32, (8, BLK), 0)
    scalars[...] = jnp.where(row == 0, phibar, jnp.where(row == 1, rhobar, beta[0]))


def end_kernel(half, other, x, w, scalars, out, residual):
    beta = jnp.sqrt(half[:1, :] + other[:1, :])
    phibar, rhobar, beta_first = scalars[:1, :], scalars[1:2, :], scalars[2:3, :]
    rho = jnp.sqrt(rhobar * rhobar + beta * beta)
    out[...] = x[...] + rhobar / rho * phibar / rho * w[...]
    residual[...] = (beta / rho * phibar / beta_first)[:, :1]


def split_tiles(blocks, blk_row, blk_col, rhs, place):
    rows = blocks.shape[0]
    vmem = pl.BlockSpec(memory_space=pltpu.VMEM)
    there = [pltpu.with_memory_space_constraint(x, pltpu.HBM) for x in (blocks, blk_row, blk_col, rhs)]
    return pl.pallas_call(
        tiles_kernel,
        out_shape=[
            pltpu.VMEM((2 * rows, 2 * BLK), bf16),
            jax.ShapeDtypeStruct((8, BLK), f32),
            jax.ShapeDtypeStruct((2 * NB_DEV, BLK), f32),
            jax.ShapeDtypeStruct(rhs.shape, f32),
        ],
        in_specs=[pl.BlockSpec(memory_space=pl.ANY)] * 4 + [vmem],
        out_specs=[vmem] * 4,
        scratch_shapes=[
            pltpu.VMEM((rows, BLK), f32),
            pltpu.VMEM((1, NB_DEV), jnp.int32),
            pltpu.VMEM((1, NB_DEV), jnp.int32),
            pltpu.SemaphoreType.DMA((PARTS + 3,)),
        ],
        compiler_params=pltpu.CompilerParams(vmem_limit_bytes=VMEM_LIMIT),
        cost_estimate=pl.CostEstimate(flops=0, bytes_accessed=4 * rows * BLK, transcendentals=0),
    )(*there, place)


def call(body, tiles, ins, outs):
    if tiles is not None:
        ins = [pltpu.with_memory_space_constraint(tiles, pltpu.VMEM)] + ins
    return pl.pallas_call(
        body,
        out_shape=[jax.ShapeDtypeStruct(s, f32) for s in outs],
        in_specs=[pl.BlockSpec(memory_space=pltpu.VMEM)] * len(ins),
        out_specs=[pl.BlockSpec(memory_space=pltpu.VMEM)] * len(outs),
        compiler_params=pltpu.CompilerParams(vmem_limit_bytes=VMEM_LIMIT),
    )(*ins)


def chip_steps(chips):
    if chips == 8:
        return 1, [(2, 4), (3, 5), (6, 7)]
    return 1, [(m, m + 1) for m in range(2, chips, 2)]


def on_device(n_row, n_col, rhs, blocks, blk_row, blk_col):
    chips = n_row // 2
    near, steps = chip_steps(chips)
    per_rhs = rhs.shape[0] // BLK
    per_out = COLB_DEV // n_row
    row, col = lax.axis_index("row"), lax.axis_index("col")

    def swap(x):
        return lax.ppermute(x, "row", [(r, r ^ 1) for r in range(n_row)])

    def to_near(x):
        return lax.ppermute(x, "row", [(r, r ^ (2 * near)) for r in range(n_row)])

    def to_chips(x):
        return [
            lax.ppermute(x, "row", [(r, r ^ (2 * step[r % 2])) for r in range(n_row)]) for step in steps
        ]

    def around_col(x):
        return [x] + [
            lax.ppermute(x, "col", [(i, (i - s) % n_col) for i in range(n_col)]) for s in range(1, n_col)
        ]

    rhs = rhs.reshape(per_rhs, BLK)
    pieces = around_col(rhs)
    place = jnp.full((8, BLK), col * per_rhs).astype(f32)
    tiles, consts, ats, pieces[0] = split_tiles(
        blocks.reshape(NB_DEV * BLK, BLK), blk_row.reshape(1, NB_DEV), blk_col.reshape(1, NB_DEV), rhs, place
    )
    lane = lax.broadcasted_iota(jnp.int32, (MSG - NB_DEV, BLK), 1)
    end_row = lax.broadcasted_iota(jnp.int32, (MSG - NB_DEV, BLK), 0)

    def gather(msg):
        peer, beside = swap(msg), to_near(msg)
        a, b = msg[NB_DEV:], peer[NB_DEV:]
        end = jnp.where(end_row == 0, jnp.where(lane < NB_DEV, a, b), a + b)
        both = jnp.concatenate([msg[:NB_DEV], peer[:NB_DEV], end])
        (half,) = call(gather_sum_kernel, tiles, [msg, beside] + to_chips(both), [(COLB_DEV + 8, BLK)])
        return half, swap(half)

    u_raw, msg = call(
        functools.partial(first_kernel, n_col),
        tiles,
        pieces + [consts, ats],
        [(ROWS_HELD, BLK), (MSG, BLK)],
    )
    alphas, betas, v_raws = [], [], []
    for step in range(ITERS):
        half, other = gather(msg)
        before = [v_raws[-1], alphas[-1]] if step else []
        v_raw, msg, beta = call(
            functools.partial(v_kernel, step > 0),
            tiles,
            [half, other] + before + [consts, ats],
            [(COLB_DEV, BLK), (MSG, BLK), (8, BLK)],
        )
        v_raws.append(v_raw)
        betas.append(beta)
        last = step + 1 == ITERS
        ins = [consts, u_raw, beta] + around_col(msg)
        body = functools.partial(u_kernel, n_col, last)
        if last:
            square, alpha = call(body, None, ins, [(8, BLK), (8, BLK)])
        else:
            u_raw, msg, alpha = call(
                body, tiles, ins + [ats], [(ROWS_HELD, BLK), (MSG, BLK), (8, BLK)]
            )
        alphas.append(alpha)

    mine = [lax.dynamic_slice_in_dim(v, row * per_out, per_out) for v in v_raws]
    held = call(before_end_kernel, None, mine + alphas + betas, [(per_out, BLK), (per_out, BLK), (8, BLK)])
    beside = to_near(square)
    half = functools.reduce(lambda a, b: a + b, to_chips(square + swap(square)), square + beside)
    out, residual = call(end_kernel, None, [half, swap(half), *held], [(per_out, BLK), (1, 1)])
    return out.reshape(per_out * BLK), residual.reshape(())


def solution(mesh):
    return jax.shard_map(
        functools.partial(on_device, mesh.shape["row"], mesh.shape["col"]),
        mesh=mesh,
        in_specs=(
            P(("row", "col")),
            P("row", "col", None, None, None),
            P("row", "col", None),
            P("row", "col", None),
        ),
        out_specs=(P(("col", "row")), P()),
        check_vma=False,
    )
```

```python
import functools

import jax
import jax.numpy as jnp
from jax import lax
from jax.experimental import pallas as pl
from jax.experimental.pallas import tpu as pltpu
from jax.sharding import PartitionSpec as P

BLK = 128
ROWB_DEV = 496
COLB_DEV = 512
NB_DEV = 64
ITERS = 3
MSG = NB_DEV + 8
INDEX, SQUARE = NB_DEV, NB_DEV + 1
COL_ROW, ROW_ROW, SHIFT = (slice(k, k + 1) for k in range(3))
ROWS_HELD = 512
PARTS = 8
VMEM_LIMIT = 16 * 1024 * 1024

f32 = jnp.float32
bf16 = jnp.bfloat16


def total(x):
    s = jnp.sum(jnp.sum(x, axis=0, keepdims=True), axis=1, keepdims=True)
    return jnp.broadcast_to(s, (1, BLK))


def halves(x):
    high = x.astype(bf16)
    return high, (x - high.astype(f32)).astype(bf16)


def place_sum(index_row, parts, rows):
    k = parts.shape[0]
    at = lax.broadcasted_iota(jnp.int32, (rows, k), 0).astype(f32)
    hot = jnp.where(at == index_row, 1.0, 0.0).astype(bf16)
    out = jnp.dot(hot, jnp.concatenate(halves(parts), axis=1), preferred_element_type=f32)
    return out[:, :BLK] + out[:, BLK:]


def pick(at, x):
    rows = x.shape[0]
    lane = lax.broadcasted_iota(jnp.int32, (NB_DEV, rows), 1).astype(f32)
    hot = jnp.where(lane == jnp.concatenate([at] * (rows // BLK), axis=1), 1.0, 0.0).astype(bf16)
    return jnp.dot(hot, jnp.concatenate(halves(x), axis=1), preferred_element_type=f32)


def times_tiles(tiles, first, picked, msg):
    per = 8
    row = lax.broadcasted_iota(jnp.int32, (2 * per, BLK), 0)
    for g in range(0, NB_DEV, per):
        both = jnp.concatenate([picked[g : g + per, :BLK], picked[g : g + per, BLK:]], axis=0)
        lhs = jnp.concatenate([jnp.where(row % per == t, both, 0.0) for t in range(per)], axis=1).astype(bf16)
        out = jnp.dot(lhs, tiles[(first + g) * BLK : (first + g + per) * BLK, :], preferred_element_type=f32)
        out = out[:, :BLK] + out[:, BLK:]
        msg[g : g + per, :] = out[:per] + out[per:]


def write_end(msg, index_row, square):
    row = lax.broadcasted_iota(jnp.int32, (MSG - NB_DEV, BLK), 0)
    msg[NB_DEV:, :] = jnp.where(row == 0, index_row, jnp.where(row == 1, square, 0.0))


def tiles_kernel(blocks, blk_row, blk_col, rhs, place, out, consts, ats, mine, held, rows_held, cols_held, sems):
    per = held.shape[0] // PARTS
    few = [
        pltpu.make_async_copy(a, b, sems.at[PARTS + k])
        for k, (a, b) in enumerate(((blk_row, rows_held), (blk_col, cols_held), (rhs, mine)))
    ]
    parts = [
        pltpu.make_async_copy(blocks.at[pl.ds(k * per, per)], held.at[pl.ds(k * per, per)], sems.at[k])
        for k in range(PARTS)
    ]
    for part in few + parts:
        part.start()
    for part in few:
        part.wait()
    rows, cols = rows_held[...].astype(f32), cols_held[...].astype(f32)
    shift = place[:1, :]
    consts[COL_ROW, :] = jnp.concatenate([cols, cols], axis=1)
    consts[ROW_ROW, :] = jnp.concatenate([rows, rows], axis=1)
    consts[SHIFT, :] = shift
    consts[3:, :] = jnp.zeros((5, BLK), f32)
    turned = rows - shift[:, :NB_DEV]
    turned = jnp.where(turned < 0, turned + ROWB_DEV, turned)
    ats[...] = jnp.broadcast_to(jnp.concatenate([turned, cols], axis=1), (2 * NB_DEV, BLK)).T
    for k, part in enumerate(parts):
        part.wait()
        for at in range(k * per, (k + 1) * per, BLK):
            for lane, half in zip((0, BLK), halves(held[at : at + BLK, :])):
                out[at : at + BLK, lane : lane + BLK] = half
                out[held.shape[0] + at : held.shape[0] + at + BLK, lane : lane + BLK] = half.T


def first_kernel(n_col, tiles, *refs):
    pieces, (consts, ats, u_raw, msg) = refs[:n_col], refs[n_col:]
    per = pieces[0].shape[0]
    for k, piece in enumerate(pieces):
        u_raw[k * per : (k + 1) * per, :] = piece[...]
    u_raw[ROWB_DEV:, :] = jnp.zeros((ROWS_HELD - ROWB_DEV, BLK), f32)
    u = u_raw[...]
    times_tiles(tiles, 0, pick(ats[:NB_DEV, :], u), msg)
    write_end(msg, consts[COL_ROW, :], total(u * u))


def gather_sum_kernel(tiles, own, near, *refs):
    *chips, out = refs
    lane = lax.broadcasted_iota(jnp.int32, (1, BLK), 1)
    parts = [own[:NB_DEV], near[:NB_DEV]]
    index = [jnp.where(lane < NB_DEV, own[INDEX : INDEX + 1], near[INDEX : INDEX + 1])]
    square = own[SQUARE : SQUARE + 1] + near[SQUARE : SQUARE + 1]
    n = 2 * NB_DEV
    for chip in chips:
        parts.append(chip[:n])
        index.append(chip[n : n + 1])
        square = square + chip[n + 1 : n + 2]
    out[:COLB_DEV, :] = place_sum(jnp.concatenate(index, axis=1), jnp.concatenate(parts, axis=0), COLB_DEV)
    out[COLB_DEV:, :] = jnp.broadcast_to(square, (8, BLK))


def v_kernel(has_before, tiles, half, other, *refs):
    if has_before:
        v_raw_before, alpha, consts, ats, v_raw, msg, beta_out = refs
    else:
        consts, ats, v_raw, msg, beta_out = refs
    beta = jnp.sqrt(half[COLB_DEV : COLB_DEV + 1, :] + other[COLB_DEV : COLB_DEV + 1, :])
    v = (half[:COLB_DEV, :] + other[:COLB_DEV, :]) / beta
    if has_before:
        v = v - v_raw_before[...] * (beta / alpha[:1, :])
    v_raw[...] = v
    beta_out[...] = jnp.broadcast_to(beta, (8, BLK))
    times_tiles(tiles, NB_DEV, pick(ats[NB_DEV:, :], v), msg)
    write_end(msg, consts[ROW_ROW, :], total(v * v))


def u_kernel(n_col, last, *refs):
    if not last:
        tiles, *refs = refs
    consts, u_raw_before, beta, *refs = refs
    pieces, refs = refs[:n_col], refs[n_col:]
    if last:
        square_out, alpha_out = refs
    else:
        ats, u_raw, msg, alpha_out = refs
    square = pieces[0][SQUARE : SQUARE + 1, :]
    for piece in pieces[1:]:
        square = square + piece[SQUARE : SQUARE + 1, :]
    alpha = jnp.sqrt(square)
    alpha_out[...] = jnp.broadcast_to(alpha, (8, BLK))
    lane = lax.broadcasted_iota(jnp.int32, (1, BLK), 1)
    index = [
        jnp.where(lane < NB_DEV, a[INDEX : INDEX + 1, :], b[INDEX : INDEX + 1, :])
        for a, b in zip(pieces[::2], pieces[1::2])
    ]
    index = jnp.concatenate([i - consts[SHIFT, :] for i in index], axis=1)
    index = jnp.where(index < 0, index + ROWB_DEV, index)
    prods = jnp.concatenate([piece[:NB_DEV, :] for piece in pieces], axis=0)
    front = place_sum(index, prods, ROWS_HELD)
    u = front / alpha - u_raw_before[...] * (alpha / beta[:1, :])
    square = total(u * u)
    if last:
        square_out[...] = jnp.broadcast_to(square, (8, BLK))
        return
    u_raw[...] = u
    times_tiles(tiles, 0, pick(ats[:NB_DEV, :], u), msg)
    write_end(msg, consts[COL_ROW, :], square)


def before_end_kernel(*refs):
    v_raws, alphas, betas = refs[:ITERS], refs[ITERS : 2 * ITERS], refs[2 * ITERS : 3 * ITERS]
    x_out, w_out, scalars = refs[3 * ITERS :]
    alpha = [a[:1, :] for a in alphas]
    beta = [b[:1, :] for b in betas]
    phibar, rhobar = beta[0], alpha[0]
    x = jnp.zeros(x_out.shape, f32)
    w = v_raws[0][...] / alpha[0]
    for k in range(1, ITERS):
        rho = jnp.sqrt(rhobar * rhobar + beta[k] * beta[k])
        cosine, sine = rhobar / rho, beta[k] / rho
        phi = cosine * phibar
        phibar = sine * phibar
        x = x + phi / rho * w
        w = v_raws[k][...] / alpha[k] - sine * alpha[k] / rho * w
        rhobar = -cosine * alpha[k]
    x_out[...] = x
    w_out[...] = w
    row = lax.broadcasted_iota(jnp.int32, (8, BLK), 0)
    scalars[...] = jnp.where(row == 0, phibar, jnp.where(row == 1, rhobar, beta[0]))


def end_kernel(half, other, x, w, scalars, out, residual):
    beta = jnp.sqrt(half[:1, :] + other[:1, :])
    phibar, rhobar, beta_first = scalars[:1, :], scalars[1:2, :], scalars[2:3, :]
    rho = jnp.sqrt(rhobar * rhobar + beta * beta)
    out[...] = x[...] + rhobar / rho * phibar / rho * w[...]
    residual[...] = (beta / rho * phibar / beta_first)[:, :1]


def split_tiles(blocks, blk_row, blk_col, rhs, place):
    rows = blocks.shape[0]
    vmem = pl.BlockSpec(memory_space=pltpu.VMEM)
    there = [pltpu.with_memory_space_constraint(x, pltpu.HBM) for x in (blocks, blk_row, blk_col, rhs)]
    return pl.pallas_call(
        tiles_kernel,
        out_shape=[
            pltpu.VMEM((2 * rows, 2 * BLK), bf16),
            jax.ShapeDtypeStruct((8, BLK), f32),
            jax.ShapeDtypeStruct((2 * NB_DEV, BLK), f32),
            jax.ShapeDtypeStruct(rhs.shape, f32),
        ],
        in_specs=[pl.BlockSpec(memory_space=pl.ANY)] * 4 + [vmem],
        out_specs=[vmem] * 4,
        scratch_shapes=[
            pltpu.VMEM((rows, BLK), f32),
            pltpu.VMEM((1, NB_DEV), jnp.int32),
            pltpu.VMEM((1, NB_DEV), jnp.int32),
            pltpu.SemaphoreType.DMA((PARTS + 3,)),
        ],
        compiler_params=pltpu.CompilerParams(vmem_limit_bytes=VMEM_LIMIT),
        cost_estimate=pl.CostEstimate(flops=0, bytes_accessed=4 * rows * BLK, transcendentals=0),
    )(*there, place)


def call(body, tiles, ins, outs):
    if tiles is not None:
        ins = [pltpu.with_memory_space_constraint(tiles, pltpu.VMEM)] + ins
    return pl.pallas_call(
        body,
        out_shape=[jax.ShapeDtypeStruct(s, f32) for s in outs],
        in_specs=[pl.BlockSpec(memory_space=pltpu.VMEM)] * len(ins),
        out_specs=[pl.BlockSpec(memory_space=pltpu.VMEM)] * len(outs),
        compiler_params=pltpu.CompilerParams(vmem_limit_bytes=VMEM_LIMIT),
    )(*ins)


def chip_steps(chips):
    if chips == 8:
        return (2, [(1, 7), (3, 5), (6, 4)]), (1, [(2, 4), (3, 5), (6, 7)])
    steps = 1, [(m, m + 1) for m in range(2, chips, 2)]
    return steps, steps


def on_device(n_row, n_col, rhs, blocks, blk_row, blk_col):
    chips = n_row // 2
    gather_steps, sum_steps = chip_steps(chips)
    per_rhs = rhs.shape[0] // BLK
    per_out = COLB_DEV // n_row
    row, col = lax.axis_index("row"), lax.axis_index("col")

    def swap(x):
        return lax.ppermute(x, "row", [(r, r ^ 1) for r in range(n_row)])

    def to_near(x, steps):
        return lax.ppermute(x, "row", [(r, r ^ (2 * steps[0])) for r in range(n_row)])

    def to_chips(x, steps):
        return [lax.ppermute(x, "row", [(r, r ^ (2 * step[r % 2])) for r in range(n_row)]) for step in steps[1]]

    def around_col(x):
        return [x] + [
            lax.ppermute(x, "col", [(i, (i - s) % n_col) for i in range(n_col)]) for s in range(1, n_col)
        ]

    rhs = rhs.reshape(per_rhs, BLK)
    pieces = around_col(rhs)
    place = jnp.full((8, BLK), col * per_rhs).astype(f32)
    tiles, consts, ats, pieces[0] = split_tiles(
        blocks.reshape(NB_DEV * BLK, BLK), blk_row.reshape(1, NB_DEV), blk_col.reshape(1, NB_DEV), rhs, place
    )
    lane = lax.broadcasted_iota(jnp.int32, (MSG - NB_DEV, BLK), 1)
    end_row = lax.broadcasted_iota(jnp.int32, (MSG - NB_DEV, BLK), 0)

    def gather(msg):
        peer, beside = swap(msg), to_near(jnp.pad(msg, ((0, MSG), (0, 0))), gather_steps)
        a, b = msg[NB_DEV:], peer[NB_DEV:]
        end = jnp.where(end_row == 0, jnp.where(lane < NB_DEV, a, b), a + b)
        both = jnp.concatenate([msg[:NB_DEV], peer[:NB_DEV], end])
        (half,) = call(gather_sum_kernel, tiles, [msg, beside] + to_chips(both, gather_steps), [(COLB_DEV + 8, BLK)])
        return half, swap(half)

    u_raw, msg = call(
        functools.partial(first_kernel, n_col),
        tiles,
        pieces + [consts, ats],
        [(ROWS_HELD, BLK), (MSG, BLK)],
    )
    alphas, betas, v_raws = [], [], []
    for step in range(ITERS):
        half, other = gather(msg)
        before = [v_raws[-1], alphas[-1]] if step else []
        v_raw, msg, beta = call(
            functools.partial(v_kernel, step > 0),
            tiles,
            [half, other] + before + [consts, ats],
            [(COLB_DEV, BLK), (MSG, BLK), (8, BLK)],
        )
        v_raws.append(v_raw)
        betas.append(beta)
        last = step + 1 == ITERS
        ins = [consts, u_raw, beta] + around_col(msg)
        body = functools.partial(u_kernel, n_col, last)
        if last:
            square, alpha = call(body, None, ins, [(8, BLK), (8, BLK)])
        else:
            u_raw, msg, alpha = call(
                body, tiles, ins + [ats], [(ROWS_HELD, BLK), (MSG, BLK), (8, BLK)]
            )
        alphas.append(alpha)

    mine = [lax.dynamic_slice_in_dim(v, row * per_out, per_out) for v in v_raws]
    held = call(before_end_kernel, None, mine + alphas + betas, [(per_out, BLK), (per_out, BLK), (8, BLK)])
    beside = to_near(square, sum_steps)
    half = functools.reduce(lambda a, b: a + b, to_chips(square + swap(square), sum_steps), square + beside)
    out, residual = call(end_kernel, None, [half, swap(half), *held], [(per_out, BLK), (1, 1)])
    return out.reshape(per_out * BLK), residual.reshape(())


def solution(mesh):
    return jax.shard_map(
        functools.partial(on_device, mesh.shape["row"], mesh.shape["col"]),
        mesh=mesh,
        in_specs=(
            P(("row", "col")),
            P("row", "col", None, None, None),
            P("row", "col", None),
            P("row", "col", None),
        ),
        out_specs=(P(("col", "row")), P()),
        check_vma=False,
    )
```

```python
import functools

import jax
import jax.numpy as jnp
from jax import lax
from jax.experimental import pallas as pl
from jax.experimental.pallas import tpu as pltpu
from jax.sharding import PartitionSpec as P

BLK = 128
ROWB_DEV = 496
COLB_DEV = 512
NB_DEV = 64
ITERS = 3
MSG = NB_DEV + 8
INDEX, SQUARE = NB_DEV, NB_DEV + 1
COL_ROW, ROW_ROW, SHIFT = (slice(k, k + 1) for k in range(3))
ROWS_HELD = 512
PARTS = 8
VMEM_LIMIT = 16 * 1024 * 1024

f32 = jnp.float32
bf16 = jnp.bfloat16


def total(x):
    s = jnp.sum(jnp.sum(x, axis=0, keepdims=True), axis=1, keepdims=True)
    return jnp.broadcast_to(s, (1, BLK))


def halves(x):
    high = x.astype(bf16)
    return high, (x - high.astype(f32)).astype(bf16)


def place_sum(index_row, parts, rows):
    k = parts.shape[0]
    at = lax.broadcasted_iota(jnp.int32, (rows, k), 0).astype(f32)
    hot = jnp.where(at == index_row, 1.0, 0.0).astype(bf16)
    out = jnp.dot(hot, jnp.concatenate(halves(parts), axis=1), preferred_element_type=f32)
    return out[:, :BLK] + out[:, BLK:]


def pick(at, x):
    rows = x.shape[0]
    lane = lax.broadcasted_iota(jnp.int32, (NB_DEV, rows), 1).astype(f32)
    hot = jnp.where(lane == jnp.concatenate([at] * (rows // BLK), axis=1), 1.0, 0.0).astype(bf16)
    return jnp.dot(hot, jnp.concatenate(halves(x), axis=1), preferred_element_type=f32)


def times_tiles(tiles, first, picked, msg):
    per = 8
    row = lax.broadcasted_iota(jnp.int32, (2 * per, BLK), 0)
    for g in range(0, NB_DEV, per):
        both = jnp.concatenate([picked[g : g + per, :BLK], picked[g : g + per, BLK:]], axis=0)
        lhs = jnp.concatenate([jnp.where(row % per == t, both, 0.0) for t in range(per)], axis=1).astype(bf16)
        out = jnp.dot(lhs, tiles[(first + g) * BLK : (first + g + per) * BLK, :], preferred_element_type=f32)
        out = out[:, :BLK] + out[:, BLK:]
        msg[g : g + per, :] = out[:per] + out[per:]


def write_end(msg, index_row, square):
    row = lax.broadcasted_iota(jnp.int32, (MSG - NB_DEV, BLK), 0)
    msg[NB_DEV:, :] = jnp.where(row == 0, index_row, jnp.where(row == 1, square, 0.0))


def tiles_kernel(blocks, blk_row, blk_col, rhs, place, out, consts, ats, mine, held, rows_held, cols_held, sems):
    per = held.shape[0] // PARTS
    few = [
        pltpu.make_async_copy(a, b, sems.at[PARTS + k])
        for k, (a, b) in enumerate(((blk_row, rows_held), (blk_col, cols_held), (rhs, mine)))
    ]
    parts = [
        pltpu.make_async_copy(blocks.at[pl.ds(k * per, per)], held.at[pl.ds(k * per, per)], sems.at[k])
        for k in range(PARTS)
    ]
    for part in few + parts:
        part.start()
    for part in few:
        part.wait()
    rows, cols = rows_held[...].astype(f32), cols_held[...].astype(f32)
    shift = place[:1, :]
    consts[COL_ROW, :] = jnp.concatenate([cols, cols], axis=1)
    consts[ROW_ROW, :] = jnp.concatenate([rows, rows], axis=1)
    consts[SHIFT, :] = shift
    consts[3:, :] = jnp.zeros((5, BLK), f32)
    turned = rows - shift[:, :NB_DEV]
    turned = jnp.where(turned < 0, turned + ROWB_DEV, turned)
    ats[...] = jnp.broadcast_to(jnp.concatenate([turned, cols], axis=1), (2 * NB_DEV, BLK)).T
    for k, part in enumerate(parts):
        part.wait()
        for at in range(k * per, (k + 1) * per, BLK):
            for lane, half in zip((0, BLK), halves(held[at : at + BLK, :])):
                out[at : at + BLK, lane : lane + BLK] = half
                out[held.shape[0] + at : held.shape[0] + at + BLK, lane : lane + BLK] = half.T


def first_kernel(n_col, tiles, *refs):
    pieces, (consts, ats, u_raw, msg) = refs[:n_col], refs[n_col:]
    per = pieces[0].shape[0]
    for k, piece in enumerate(pieces):
        u_raw[k * per : (k + 1) * per, :] = piece[...]
    u_raw[ROWB_DEV:, :] = jnp.zeros((ROWS_HELD - ROWB_DEV, BLK), f32)
    u = u_raw[...]
    times_tiles(tiles, 0, pick(ats[:NB_DEV, :], u), msg)
    write_end(msg, consts[COL_ROW, :], total(u * u))


def sum_messages(cores, chips):
    lane = lax.broadcasted_iota(jnp.int32, (1, BLK), 1)
    n = 2 * NB_DEV
    parts, index, square = [], [], jnp.zeros((1, BLK), f32)
    for a, b in zip(cores[::2], cores[1::2]):
        parts += [a[:NB_DEV], b[:NB_DEV]]
        index.append(jnp.where(lane < NB_DEV, a[INDEX : INDEX + 1], b[INDEX : INDEX + 1]))
        square = square + (a[SQUARE : SQUARE + 1] + b[SQUARE : SQUARE + 1])
    for chip in chips:
        parts.append(chip[:n])
        index.append(chip[n : n + 1])
        square = square + chip[n + 1 : n + 2]
    return place_sum(jnp.concatenate(index, axis=1), jnp.concatenate(parts, axis=0), COLB_DEV), square


def early_kernel(n_cores, *refs):
    *msgs, out = refs
    back, square = sum_messages(msgs[:n_cores], msgs[n_cores:])
    out[:COLB_DEV, :] = back
    out[COLB_DEV:, :] = jnp.broadcast_to(square, (8, BLK))


def v_kernel(has_before, n_msgs, tiles, *refs):
    msgs, refs = refs[:n_msgs], refs[n_msgs:]
    if has_before:
        v_raw_before, alpha, consts, ats, v_raw, msg, beta_out = refs
    else:
        consts, ats, v_raw, msg, beta_out = refs
    early, *chips = msgs
    back, square = sum_messages([], chips)
    beta = jnp.sqrt(early[COLB_DEV : COLB_DEV + 1, :] + square)
    v = (early[:COLB_DEV, :] + back) / beta
    if has_before:
        v = v - v_raw_before[...] * (beta / alpha[:1, :])
    v_raw[...] = v
    beta_out[...] = jnp.broadcast_to(beta, (8, BLK))
    times_tiles(tiles, NB_DEV, pick(ats[NB_DEV:, :], v), msg)
    write_end(msg, consts[ROW_ROW, :], total(v * v))


def u_kernel(n_col, last, *refs):
    if not last:
        tiles, *refs = refs
    consts, u_raw_before, beta, *refs = refs
    pieces, refs = refs[:n_col], refs[n_col:]
    if last:
        square_out, alpha_out = refs
    else:
        ats, u_raw, msg, alpha_out = refs
    square = pieces[0][SQUARE : SQUARE + 1, :]
    for piece in pieces[1:]:
        square = square + piece[SQUARE : SQUARE + 1, :]
    alpha = jnp.sqrt(square)
    alpha_out[...] = jnp.broadcast_to(alpha, (8, BLK))
    lane = lax.broadcasted_iota(jnp.int32, (1, BLK), 1)
    index = [
        jnp.where(lane < NB_DEV, a[INDEX : INDEX + 1, :], b[INDEX : INDEX + 1, :])
        for a, b in zip(pieces[::2], pieces[1::2])
    ]
    index = jnp.concatenate([i - consts[SHIFT, :] for i in index], axis=1)
    index = jnp.where(index < 0, index + ROWB_DEV, index)
    prods = jnp.concatenate([piece[:NB_DEV, :] for piece in pieces], axis=0)
    front = place_sum(index, prods, ROWS_HELD)
    u = front / alpha - u_raw_before[...] * (alpha / beta[:1, :])
    square = total(u * u)
    if last:
        square_out[...] = jnp.broadcast_to(square, (8, BLK))
        return
    u_raw[...] = u
    times_tiles(tiles, 0, pick(ats[:NB_DEV, :], u), msg)
    write_end(msg, consts[COL_ROW, :], square)


def before_end_kernel(*refs):
    v_raws, alphas, betas = refs[:ITERS], refs[ITERS : 2 * ITERS], refs[2 * ITERS : 3 * ITERS]
    x_out, w_out, scalars = refs[3 * ITERS :]
    alpha = [a[:1, :] for a in alphas]
    beta = [b[:1, :] for b in betas]
    phibar, rhobar = beta[0], alpha[0]
    x = jnp.zeros(x_out.shape, f32)
    w = v_raws[0][...] / alpha[0]
    for k in range(1, ITERS):
        rho = jnp.sqrt(rhobar * rhobar + beta[k] * beta[k])
        cosine, sine = rhobar / rho, beta[k] / rho
        phi = cosine * phibar
        phibar = sine * phibar
        x = x + phi / rho * w
        w = v_raws[k][...] / alpha[k] - sine * alpha[k] / rho * w
        rhobar = -cosine * alpha[k]
    x_out[...] = x
    w_out[...] = w
    row = lax.broadcasted_iota(jnp.int32, (8, BLK), 0)
    scalars[...] = jnp.where(row == 0, phibar, jnp.where(row == 1, rhobar, beta[0]))


def end_kernel(half, other, x, w, scalars, out, residual):
    beta = jnp.sqrt(half[:1, :] + other[:1, :])
    phibar, rhobar, beta_first = scalars[:1, :], scalars[1:2, :], scalars[2:3, :]
    rho = jnp.sqrt(rhobar * rhobar + beta * beta)
    out[...] = x[...] + rhobar / rho * phibar / rho * w[...]
    residual[...] = (beta / rho * phibar / beta_first)[:, :1]


def split_tiles(blocks, blk_row, blk_col, rhs, place):
    rows = blocks.shape[0]
    vmem = pl.BlockSpec(memory_space=pltpu.VMEM)
    there = [pltpu.with_memory_space_constraint(x, pltpu.HBM) for x in (blocks, blk_row, blk_col, rhs)]
    return pl.pallas_call(
        tiles_kernel,
        out_shape=[
            pltpu.VMEM((2 * rows, 2 * BLK), bf16),
            jax.ShapeDtypeStruct((8, BLK), f32),
            jax.ShapeDtypeStruct((2 * NB_DEV, BLK), f32),
            jax.ShapeDtypeStruct(rhs.shape, f32),
        ],
        in_specs=[pl.BlockSpec(memory_space=pl.ANY)] * 4 + [vmem],
        out_specs=[vmem] * 4,
        scratch_shapes=[
            pltpu.VMEM((rows, BLK), f32),
            pltpu.VMEM((1, NB_DEV), jnp.int32),
            pltpu.VMEM((1, NB_DEV), jnp.int32),
            pltpu.SemaphoreType.DMA((PARTS + 3,)),
        ],
        compiler_params=pltpu.CompilerParams(vmem_limit_bytes=VMEM_LIMIT),
        cost_estimate=pl.CostEstimate(flops=0, bytes_accessed=4 * rows * BLK, transcendentals=0),
    )(*there, place)


def call(body, tiles, ins, outs):
    if tiles is not None:
        ins = [pltpu.with_memory_space_constraint(tiles, pltpu.VMEM)] + ins
    return pl.pallas_call(
        body,
        out_shape=[jax.ShapeDtypeStruct(s, f32) for s in outs],
        in_specs=[pl.BlockSpec(memory_space=pltpu.VMEM)] * len(ins),
        out_specs=[pl.BlockSpec(memory_space=pltpu.VMEM)] * len(outs),
        compiler_params=pltpu.CompilerParams(vmem_limit_bytes=VMEM_LIMIT),
    )(*ins)


def chip_steps(chips):
    if chips == 8:
        return (2, [(1, 7), (3, 5), (6, 4)]), (1, [(2, 4), (3, 5), (6, 7)])
    steps = 1, [(m, m + 1) for m in range(2, chips, 2)]
    return steps, steps


def on_device(n_row, n_col, rhs, blocks, blk_row, blk_col):
    chips = n_row // 2
    gather_steps, sum_steps = chip_steps(chips)
    per_rhs = rhs.shape[0] // BLK
    per_out = COLB_DEV // n_row
    row, col = lax.axis_index("row"), lax.axis_index("col")

    def swap(x):
        return lax.ppermute(x, "row", [(r, r ^ 1) for r in range(n_row)])

    def to_near(x, steps):
        return lax.ppermute(x, "row", [(r, r ^ (2 * steps[0])) for r in range(n_row)])

    def to_chips(x, steps):
        return [lax.ppermute(x, "row", [(r, r ^ (2 * step[r % 2])) for r in range(n_row)]) for step in steps[1]]

    def around_col(x):
        return [x] + [
            lax.ppermute(x, "col", [(i, (i - s) % n_col) for i in range(n_col)]) for s in range(1, n_col)
        ]

    rhs = rhs.reshape(per_rhs, BLK)
    pieces = around_col(rhs)
    place = jnp.full((8, BLK), col * per_rhs).astype(f32)
    tiles, consts, ats, pieces[0] = split_tiles(
        blocks.reshape(NB_DEV * BLK, BLK), blk_row.reshape(1, NB_DEV), blk_col.reshape(1, NB_DEV), rhs, place
    )
    lane = lax.broadcasted_iota(jnp.int32, (MSG - NB_DEV, BLK), 1)
    end_row = lax.broadcasted_iota(jnp.int32, (MSG - NB_DEV, BLK), 0)

    def gather(msg):
        peer, beside = swap(msg), to_near(jnp.pad(msg, ((0, MSG), (0, 0))), gather_steps)
        a, b = msg[NB_DEV:], peer[NB_DEV:]
        end = jnp.where(end_row == 0, jnp.where(lane < NB_DEV, a, b), a + b)
        both = jnp.concatenate([msg[:NB_DEV], peer[:NB_DEV], end])
        chips = to_chips(both, gather_steps)
        chips = [(c, swap(c)) for c in chips]
        late, soon = sum(chips[:1], ()), sum(chips[1:], ())
        (early,) = call(
            functools.partial(early_kernel, 4), None, [msg, peer, beside, swap(beside), *soon], [(COLB_DEV + 8, BLK)]
        )
        return [early, *late]

    u_raw, msg = call(
        functools.partial(first_kernel, n_col),
        tiles,
        pieces + [consts, ats],
        [(ROWS_HELD, BLK), (MSG, BLK)],
    )
    alphas, betas, v_raws = [], [], []
    for step in range(ITERS):
        msgs = gather(msg)
        before = [v_raws[-1], alphas[-1]] if step else []
        v_raw, msg, beta = call(
            functools.partial(v_kernel, step > 0, len(msgs)),
            tiles,
            msgs + before + [consts, ats],
            [(COLB_DEV, BLK), (MSG, BLK), (8, BLK)],
        )
        v_raws.append(v_raw)
        betas.append(beta)
        last = step + 1 == ITERS
        ins = [consts, u_raw, beta] + around_col(msg)
        body = functools.partial(u_kernel, n_col, last)
        if last:
            square, alpha = call(body, None, ins, [(8, BLK), (8, BLK)])
        else:
            u_raw, msg, alpha = call(
                body, tiles, ins + [ats], [(ROWS_HELD, BLK), (MSG, BLK), (8, BLK)]
            )
        alphas.append(alpha)

    mine = [lax.dynamic_slice_in_dim(v, row * per_out, per_out) for v in v_raws]
    held = call(before_end_kernel, None, mine + alphas + betas, [(per_out, BLK), (per_out, BLK), (8, BLK)])
    beside = to_near(square, sum_steps)
    half = functools.reduce(lambda a, b: a + b, to_chips(square + swap(square), sum_steps), square + beside)
    out, residual = call(end_kernel, None, [half, swap(half), *held], [(per_out, BLK), (1, 1)])
    return out.reshape(per_out * BLK), residual.reshape(())


def solution(mesh):
    return jax.shard_map(
        functools.partial(on_device, mesh.shape["row"], mesh.shape["col"]),
        mesh=mesh,
        in_specs=(
            P(("row", "col")),
            P("row", "col", None, None, None),
            P("row", "col", None),
            P("row", "col", None),
        ),
        out_specs=(P(("col", "row")), P()),
        check_vma=False,
    )
```

```python
import functools

import jax
import jax.numpy as jnp
from jax import lax
from jax.experimental import pallas as pl
from jax.experimental.pallas import tpu as pltpu
from jax.sharding import PartitionSpec as P

BLK = 128
ROWB_DEV = 496
COLB_DEV = 512
NB_DEV = 64
ITERS = 3
MSG = NB_DEV + 8
INDEX, SQUARE = NB_DEV, NB_DEV + 1
COL_ROW, ROW_ROW, SHIFT = (slice(k, k + 1) for k in range(3))
ROWS_HELD = 512
PARTS = 8
VMEM_LIMIT = 16 * 1024 * 1024

f32 = jnp.float32
bf16 = jnp.bfloat16


def total(x):
    s = jnp.sum(jnp.sum(x, axis=0, keepdims=True), axis=1, keepdims=True)
    return jnp.broadcast_to(s, (1, BLK))


def halves(x):
    high = x.astype(bf16)
    return high, (x - high.astype(f32)).astype(bf16)


def place_sum(index_row, parts, rows):
    k = parts.shape[0]
    at = lax.broadcasted_iota(jnp.int32, (rows, k), 0).astype(f32)
    hot = jnp.where(at == index_row, 1.0, 0.0).astype(bf16)
    out = jnp.dot(hot, jnp.concatenate(halves(parts), axis=1), preferred_element_type=f32)
    return out[:, :BLK] + out[:, BLK:]


def pick(at, x):
    rows = x.shape[0]
    lane = lax.broadcasted_iota(jnp.int32, (NB_DEV, rows), 1).astype(f32)
    hot = jnp.where(lane == jnp.concatenate([at] * (rows // BLK), axis=1), 1.0, 0.0).astype(bf16)
    return jnp.dot(hot, jnp.concatenate(halves(x), axis=1), preferred_element_type=f32)


def times_tiles(tiles, first, picked, msg):
    per = 8
    row = lax.broadcasted_iota(jnp.int32, (2 * per, BLK), 0)
    for g in range(0, NB_DEV, per):
        both = jnp.concatenate([picked[g : g + per, :BLK], picked[g : g + per, BLK:]], axis=0)
        lhs = jnp.concatenate([jnp.where(row % per == t, both, 0.0) for t in range(per)], axis=1).astype(bf16)
        out = jnp.dot(lhs, tiles[(first + g) * BLK : (first + g + per) * BLK, :], preferred_element_type=f32)
        out = out[:, :BLK] + out[:, BLK:]
        msg[g : g + per, :] = out[:per] + out[per:]


def write_end(msg, index_row, square):
    row = lax.broadcasted_iota(jnp.int32, (MSG - NB_DEV, BLK), 0)
    msg[NB_DEV:, :] = jnp.where(row == 0, index_row, jnp.where(row == 1, square, 0.0))


def tiles_kernel(blocks, blk_row, blk_col, rhs, place, out, consts, ats, mine, held, rows_held, cols_held, sems):
    per = held.shape[0] // PARTS
    few = [
        pltpu.make_async_copy(a, b, sems.at[PARTS + k])
        for k, (a, b) in enumerate(((blk_row, rows_held), (blk_col, cols_held), (rhs, mine)))
    ]
    parts = [
        pltpu.make_async_copy(blocks.at[pl.ds(k * per, per)], held.at[pl.ds(k * per, per)], sems.at[k])
        for k in range(PARTS)
    ]
    for part in few + parts:
        part.start()
    for part in few:
        part.wait()
    rows, cols = rows_held[...].astype(f32), cols_held[...].astype(f32)
    shift = place[:1, :]
    consts[COL_ROW, :] = jnp.concatenate([cols, cols], axis=1)
    consts[ROW_ROW, :] = jnp.concatenate([rows, rows], axis=1)
    consts[SHIFT, :] = shift
    consts[3:, :] = jnp.zeros((5, BLK), f32)
    turned = rows - shift[:, :NB_DEV]
    turned = jnp.where(turned < 0, turned + ROWB_DEV, turned)
    ats[...] = jnp.broadcast_to(jnp.concatenate([turned, cols], axis=1), (2 * NB_DEV, BLK)).T
    for k, part in enumerate(parts):
        part.wait()
        for at in range(k * per, (k + 1) * per, BLK):
            for lane, half in zip((0, BLK), halves(held[at : at + BLK, :])):
                out[at : at + BLK, lane : lane + BLK] = half
                out[held.shape[0] + at : held.shape[0] + at + BLK, lane : lane + BLK] = half.T


def first_kernel(n_col, tiles, *refs):
    pieces, (consts, ats, u_raw, msg) = refs[:n_col], refs[n_col:]
    per = pieces[0].shape[0]
    for k, piece in enumerate(pieces):
        u_raw[k * per : (k + 1) * per, :] = piece[...]
    u_raw[ROWB_DEV:, :] = jnp.zeros((ROWS_HELD - ROWB_DEV, BLK), f32)
    u = u_raw[...]
    times_tiles(tiles, 0, pick(ats[:NB_DEV, :], u), msg)
    write_end(msg, consts[COL_ROW, :], total(u * u))


def sum_messages(cores, chips):
    lane = lax.broadcasted_iota(jnp.int32, (1, BLK), 1)
    n = 2 * NB_DEV
    parts, index, square = [], [], jnp.zeros((1, BLK), f32)
    for a, b in zip(cores[::2], cores[1::2]):
        parts += [a[:NB_DEV], b[:NB_DEV]]
        index.append(jnp.where(lane < NB_DEV, a[INDEX : INDEX + 1], b[INDEX : INDEX + 1]))
        square = square + (a[SQUARE : SQUARE + 1] + b[SQUARE : SQUARE + 1])
    for chip in chips:
        parts.append(chip[:n])
        index.append(chip[n : n + 1])
        square = square + chip[n + 1 : n + 2]
    return place_sum(jnp.concatenate(index, axis=1), jnp.concatenate(parts, axis=0), COLB_DEV), square


def early_kernel(n_cores, *refs):
    *msgs, out = refs
    back, square = sum_messages(msgs[:n_cores], msgs[n_cores:])
    out[:COLB_DEV, :] = back
    out[COLB_DEV:, :] = jnp.broadcast_to(square, (8, BLK))


def v_kernel(has_before, n_msgs, tiles, *refs):
    msgs, refs = refs[:n_msgs], refs[n_msgs:]
    if has_before:
        v_raw_before, alpha, consts, ats, v_raw, msg, beta_out = refs
    else:
        consts, ats, v_raw, msg, beta_out = refs
    early, *chips = msgs
    back, square = sum_messages([], chips)
    beta = jnp.sqrt(early[COLB_DEV : COLB_DEV + 1, :] + square)
    v = (early[:COLB_DEV, :] + back) / beta
    if has_before:
        v = v - v_raw_before[...] * (beta / alpha[:1, :])
    v_raw[...] = v
    beta_out[...] = jnp.broadcast_to(beta, (8, BLK))
    times_tiles(tiles, NB_DEV, pick(ats[NB_DEV:, :], v), msg)
    write_end(msg, consts[ROW_ROW, :], total(v * v))


def u_kernel(n_col, last, *refs):
    if not last:
        tiles, *refs = refs
    consts, u_raw_before, beta, *refs = refs
    pieces, refs = refs[:n_col], refs[n_col:]
    if last:
        square_out, alpha_out = refs
    else:
        ats, u_raw, msg, alpha_out = refs
    square = pieces[0][SQUARE : SQUARE + 1, :]
    for piece in pieces[1:]:
        square = square + piece[SQUARE : SQUARE + 1, :]
    alpha = jnp.sqrt(square)
    alpha_out[...] = jnp.broadcast_to(alpha, (8, BLK))
    lane = lax.broadcasted_iota(jnp.int32, (1, BLK), 1)
    index = [
        jnp.where(lane < NB_DEV, a[INDEX : INDEX + 1, :], b[INDEX : INDEX + 1, :])
        for a, b in zip(pieces[::2], pieces[1::2])
    ]
    index = jnp.concatenate([i - consts[SHIFT, :] for i in index], axis=1)
    index = jnp.where(index < 0, index + ROWB_DEV, index)
    prods = jnp.concatenate([piece[:NB_DEV, :] for piece in pieces], axis=0)
    front = place_sum(index, prods, ROWS_HELD)
    u = front / alpha - u_raw_before[...] * (alpha / beta[:1, :])
    square = total(u * u)
    if last:
        square_out[...] = jnp.broadcast_to(square, (8, BLK))
        return
    u_raw[...] = u
    times_tiles(tiles, 0, pick(ats[:NB_DEV, :], u), msg)
    write_end(msg, consts[COL_ROW, :], square)


def before_end_kernel(*refs):
    v_raws, alphas, betas = refs[:ITERS], refs[ITERS : 2 * ITERS], refs[2 * ITERS : 3 * ITERS]
    x_out, w_out, scalars = refs[3 * ITERS :]
    alpha = [a[:1, :] for a in alphas]
    beta = [b[:1, :] for b in betas]
    phibar, rhobar = beta[0], alpha[0]
    x = jnp.zeros(x_out.shape, f32)
    w = v_raws[0][...] / alpha[0]
    for k in range(1, ITERS):
        rho = jnp.sqrt(rhobar * rhobar + beta[k] * beta[k])
        cosine, sine = rhobar / rho, beta[k] / rho
        phi = cosine * phibar
        phibar = sine * phibar
        x = x + phi / rho * w
        w = v_raws[k][...] / alpha[k] - sine * alpha[k] / rho * w
        rhobar = -cosine * alpha[k]
    x_out[...] = x
    w_out[...] = w
    row = lax.broadcasted_iota(jnp.int32, (8, BLK), 0)
    scalars[...] = jnp.where(row == 0, phibar, jnp.where(row == 1, rhobar, beta[0]))


def end_kernel(half, other, x, w, scalars, out, residual):
    beta = jnp.sqrt(half[:1, :] + other[:1, :])
    phibar, rhobar, beta_first = scalars[:1, :], scalars[1:2, :], scalars[2:3, :]
    rho = jnp.sqrt(rhobar * rhobar + beta * beta)
    out[...] = x[...] + rhobar / rho * phibar / rho * w[...]
    residual[...] = (beta / rho * phibar / beta_first)[:, :1]


def split_tiles(blocks, blk_row, blk_col, rhs, place):
    rows = blocks.shape[0]
    vmem = pl.BlockSpec(memory_space=pltpu.VMEM)
    there = [pltpu.with_memory_space_constraint(x, pltpu.HBM) for x in (blocks, blk_row, blk_col, rhs)]
    return pl.pallas_call(
        tiles_kernel,
        out_shape=[
            pltpu.VMEM((2 * rows, 2 * BLK), bf16),
            jax.ShapeDtypeStruct((8, BLK), f32),
            jax.ShapeDtypeStruct((2 * NB_DEV, BLK), f32),
            jax.ShapeDtypeStruct(rhs.shape, f32),
        ],
        in_specs=[pl.BlockSpec(memory_space=pl.ANY)] * 4 + [vmem],
        out_specs=[vmem] * 4,
        scratch_shapes=[
            pltpu.VMEM((rows, BLK), f32),
            pltpu.VMEM((1, NB_DEV), jnp.int32),
            pltpu.VMEM((1, NB_DEV), jnp.int32),
            pltpu.SemaphoreType.DMA((PARTS + 3,)),
        ],
        compiler_params=pltpu.CompilerParams(vmem_limit_bytes=VMEM_LIMIT),
        cost_estimate=pl.CostEstimate(flops=0, bytes_accessed=4 * rows * BLK, transcendentals=0),
    )(*there, place)


def call(body, tiles, ins, outs):
    if tiles is not None:
        ins = [pltpu.with_memory_space_constraint(tiles, pltpu.VMEM)] + ins
    return pl.pallas_call(
        body,
        out_shape=[jax.ShapeDtypeStruct(s, f32) for s in outs],
        in_specs=[pl.BlockSpec(memory_space=pltpu.VMEM)] * len(ins),
        out_specs=[pl.BlockSpec(memory_space=pltpu.VMEM)] * len(outs),
        compiler_params=pltpu.CompilerParams(vmem_limit_bytes=VMEM_LIMIT),
    )(*ins)


def chip_steps(chips):
    if chips == 8:
        return (2, [(3, 4), (1, 5), (6, 7)]), (1, [(2, 4), (3, 5), (6, 7)])
    steps = 1, [(m, m + 1) for m in range(2, chips, 2)]
    return steps, steps


def on_device(n_row, n_col, rhs, blocks, blk_row, blk_col):
    chips = n_row // 2
    gather_steps, sum_steps = chip_steps(chips)
    per_rhs = rhs.shape[0] // BLK
    per_out = COLB_DEV // n_row
    row, col = lax.axis_index("row"), lax.axis_index("col")

    def swap(x):
        return lax.ppermute(x, "row", [(r, r ^ 1) for r in range(n_row)])

    def to_near(x, steps):
        return lax.ppermute(x, "row", [(r, r ^ (2 * steps[0])) for r in range(n_row)])

    def to_chips(x, steps):
        return [lax.ppermute(x, "row", [(r, r ^ (2 * step[r % 2])) for r in range(n_row)]) for step in steps[1]]

    def around_col(x):
        return [x] + [
            lax.ppermute(x, "col", [(i, (i - s) % n_col) for i in range(n_col)]) for s in range(1, n_col)
        ]

    rhs = rhs.reshape(per_rhs, BLK)
    pieces = around_col(rhs)
    place = jnp.full((8, BLK), col * per_rhs).astype(f32)
    tiles, consts, ats, pieces[0] = split_tiles(
        blocks.reshape(NB_DEV * BLK, BLK), blk_row.reshape(1, NB_DEV), blk_col.reshape(1, NB_DEV), rhs, place
    )
    lane = lax.broadcasted_iota(jnp.int32, (MSG - NB_DEV, BLK), 1)
    end_row = lax.broadcasted_iota(jnp.int32, (MSG - NB_DEV, BLK), 0)

    def gather(msg):
        peer, beside = swap(msg), to_near(jnp.pad(msg, ((0, MSG), (0, 0))), gather_steps)
        a, b = msg[NB_DEV:], peer[NB_DEV:]
        end = jnp.where(end_row == 0, jnp.where(lane < NB_DEV, a, b), a + b)
        both = jnp.concatenate([msg[:NB_DEV], peer[:NB_DEV], end])
        chips = to_chips(both, gather_steps)
        chips = [(c, swap(c)) for c in chips]
        late, soon = sum(chips[:1], ()), sum(chips[1:], ())
        (early,) = call(
            functools.partial(early_kernel, 4), None, [msg, peer, beside, swap(beside), *soon], [(COLB_DEV + 8, BLK)]
        )
        return [early, *late]

    u_raw, msg = call(
        functools.partial(first_kernel, n_col),
        tiles,
        pieces + [consts, ats],
        [(ROWS_HELD, BLK), (MSG, BLK)],
    )
    alphas, betas, v_raws = [], [], []
    for step in range(ITERS):
        msgs = gather(msg)
        before = [v_raws[-1], alphas[-1]] if step else []
        v_raw, msg, beta = call(
            functools.partial(v_kernel, step > 0, len(msgs)),
            tiles,
            msgs + before + [consts, ats],
            [(COLB_DEV, BLK), (MSG, BLK), (8, BLK)],
        )
        v_raws.append(v_raw)
        betas.append(beta)
        last = step + 1 == ITERS
        ins = [consts, u_raw, beta] + around_col(msg)
        body = functools.partial(u_kernel, n_col, last)
        if last:
            square, alpha = call(body, None, ins, [(8, BLK), (8, BLK)])
        else:
            u_raw, msg, alpha = call(
                body, tiles, ins + [ats], [(ROWS_HELD, BLK), (MSG, BLK), (8, BLK)]
            )
        alphas.append(alpha)

    mine = [lax.dynamic_slice_in_dim(v, row * per_out, per_out) for v in v_raws]
    held = call(before_end_kernel, None, mine + alphas + betas, [(per_out, BLK), (per_out, BLK), (8, BLK)])
    beside = to_near(square, sum_steps)
    half = functools.reduce(lambda a, b: a + b, to_chips(square + swap(square), sum_steps), square + beside)
    out, residual = call(end_kernel, None, [half, swap(half), *held], [(per_out, BLK), (1, 1)])
    return out.reshape(per_out * BLK), residual.reshape(())


def solution(mesh):
    return jax.shard_map(
        functools.partial(on_device, mesh.shape["row"], mesh.shape["col"]),
        mesh=mesh,
        in_specs=(
            P(("row", "col")),
            P("row", "col", None, None, None),
            P("row", "col", None),
            P("row", "col", None),
        ),
        out_specs=(P(("col", "row")), P()),
        check_vma=False,
    )
```

```python
import functools

import jax
import jax.numpy as jnp
from jax import lax
from jax.experimental import pallas as pl
from jax.experimental.pallas import tpu as pltpu
from jax.sharding import PartitionSpec as P

BLK = 128
ROWB_DEV = 496
COLB_DEV = 512
NB_DEV = 64
ITERS = 3
MSG = NB_DEV + 8
INDEX, SQUARE = NB_DEV, NB_DEV + 1
COL_ROW, ROW_ROW, SHIFT = (slice(k, k + 1) for k in range(3))
ROWS_HELD = 512
PARTS = 8
VMEM_LIMIT = 16 * 1024 * 1024

f32 = jnp.float32
bf16 = jnp.bfloat16


def total(x):
    s = jnp.sum(jnp.sum(x, axis=0, keepdims=True), axis=1, keepdims=True)
    return jnp.broadcast_to(s, (1, BLK))


def halves(x):
    high = x.astype(bf16)
    return high, (x - high.astype(f32)).astype(bf16)


def place_sum(index_row, parts, rows):
    k = parts.shape[0]
    at = lax.broadcasted_iota(jnp.int32, (rows, k), 0).astype(f32)
    hot = jnp.where(at == index_row, 1.0, 0.0).astype(bf16)
    out = jnp.dot(hot, jnp.concatenate(halves(parts), axis=1), preferred_element_type=f32)
    return out[:, :BLK] + out[:, BLK:]


def pick(at, x):
    rows = x.shape[0]
    lane = lax.broadcasted_iota(jnp.int32, (NB_DEV, rows), 1).astype(f32)
    hot = jnp.where(lane == jnp.concatenate([at] * (rows // BLK), axis=1), 1.0, 0.0).astype(bf16)
    return jnp.dot(hot, jnp.concatenate(halves(x), axis=1), preferred_element_type=f32)


def times_tiles(tiles, first, picked, msg):
    per = 8
    row = lax.broadcasted_iota(jnp.int32, (2 * per, BLK), 0)
    for g in range(0, NB_DEV, per):
        both = jnp.concatenate([picked[g : g + per, :BLK], picked[g : g + per, BLK:]], axis=0)
        lhs = jnp.concatenate([jnp.where(row % per == t, both, 0.0) for t in range(per)], axis=1).astype(bf16)
        out = jnp.dot(lhs, tiles[(first + g) * BLK : (first + g + per) * BLK, :], preferred_element_type=f32)
        out = out[:, :BLK] + out[:, BLK:]
        msg[g : g + per, :] = out[:per] + out[per:]


def write_end(msg, index_row, square):
    row = lax.broadcasted_iota(jnp.int32, (MSG - NB_DEV, BLK), 0)
    msg[NB_DEV:, :] = jnp.where(row == 0, index_row, jnp.where(row == 1, square, 0.0))


def tiles_kernel(blocks, blk_row, blk_col, rhs, place, out, consts, ats, mine, held, rows_held, cols_held, sems):
    per = held.shape[0] // PARTS
    few = [
        pltpu.make_async_copy(a, b, sems.at[PARTS + k])
        for k, (a, b) in enumerate(((blk_row, rows_held), (blk_col, cols_held), (rhs, mine)))
    ]
    parts = [
        pltpu.make_async_copy(blocks.at[pl.ds(k * per, per)], held.at[pl.ds(k * per, per)], sems.at[k])
        for k in range(PARTS)
    ]
    for part in few + parts:
        part.start()
    for part in few:
        part.wait()
    rows, cols = rows_held[...].astype(f32), cols_held[...].astype(f32)
    shift = place[:1, :]
    consts[COL_ROW, :] = jnp.concatenate([cols, cols], axis=1)
    consts[ROW_ROW, :] = jnp.concatenate([rows, rows], axis=1)
    consts[SHIFT, :] = shift
    consts[3:, :] = jnp.zeros((5, BLK), f32)
    turned = rows - shift[:, :NB_DEV]
    turned = jnp.where(turned < 0, turned + ROWB_DEV, turned)
    ats[...] = jnp.broadcast_to(jnp.concatenate([turned, cols], axis=1), (2 * NB_DEV, BLK)).T
    for k, part in enumerate(parts):
        part.wait()
        for at in range(k * per, (k + 1) * per, BLK):
            for lane, half in zip((0, BLK), halves(held[at : at + BLK, :])):
                out[at : at + BLK, lane : lane + BLK] = half
                out[held.shape[0] + at : held.shape[0] + at + BLK, lane : lane + BLK] = half.T


def first_kernel(n_col, tiles, *refs):
    pieces, (consts, ats, u_raw, msg) = refs[:n_col], refs[n_col:]
    per = pieces[0].shape[0]
    for k, piece in enumerate(pieces):
        u_raw[k * per : (k + 1) * per, :] = piece[...]
    u_raw[ROWB_DEV:, :] = jnp.zeros((ROWS_HELD - ROWB_DEV, BLK), f32)
    u = u_raw[...]
    times_tiles(tiles, 0, pick(ats[:NB_DEV, :], u), msg)
    write_end(msg, consts[COL_ROW, :], total(u * u))


def sum_messages(cores, chips):
    lane = lax.broadcasted_iota(jnp.int32, (1, BLK), 1)
    n = 2 * NB_DEV
    parts, index, square = [], [], jnp.zeros((1, BLK), f32)
    for a, b in zip(cores[::2], cores[1::2]):
        parts += [a[:NB_DEV], b[:NB_DEV]]
        index.append(jnp.where(lane < NB_DEV, a[INDEX : INDEX + 1], b[INDEX : INDEX + 1]))
        square = square + (a[SQUARE : SQUARE + 1] + b[SQUARE : SQUARE + 1])
    for chip in chips:
        parts.append(chip[:n])
        index.append(chip[n : n + 1])
        square = square + chip[n + 1 : n + 2]
    return place_sum(jnp.concatenate(index, axis=1), jnp.concatenate(parts, axis=0), COLB_DEV), square


def early_kernel(n_cores, *refs):
    *msgs, out = refs
    back, square = sum_messages(msgs[:n_cores], msgs[n_cores:])
    out[:COLB_DEV, :] = back
    out[COLB_DEV:, :] = jnp.broadcast_to(square, (8, BLK))


def v_kernel(has_before, n_msgs, tiles, *refs):
    msgs, refs = refs[:n_msgs], refs[n_msgs:]
    if has_before:
        v_raw_before, alpha, consts, ats, v_raw, msg, beta_out = refs
    else:
        consts, ats, v_raw, msg, beta_out = refs
    early, *chips = msgs
    back, square = sum_messages([], chips)
    beta = jnp.sqrt(early[COLB_DEV : COLB_DEV + 1, :] + square)
    v = (early[:COLB_DEV, :] + back) / beta
    if has_before:
        v = v - v_raw_before[...] * (beta / alpha[:1, :])
    v_raw[...] = v
    beta_out[...] = jnp.broadcast_to(beta, (8, BLK))
    times_tiles(tiles, NB_DEV, pick(ats[NB_DEV:, :], v), msg)
    write_end(msg, consts[ROW_ROW, :], total(v * v))


def u_kernel(n_col, last, *refs):
    if not last:
        tiles, *refs = refs
    consts, u_raw_before, beta, *refs = refs
    pieces, refs = refs[:n_col], refs[n_col:]
    if last:
        square_out, alpha_out = refs
    else:
        ats, u_raw, msg, alpha_out = refs
    square = pieces[0][SQUARE : SQUARE + 1, :]
    for piece in pieces[1:]:
        square = square + piece[SQUARE : SQUARE + 1, :]
    alpha = jnp.sqrt(square)
    alpha_out[...] = jnp.broadcast_to(alpha, (8, BLK))
    lane = lax.broadcasted_iota(jnp.int32, (1, BLK), 1)
    index = [
        jnp.where(lane < NB_DEV, a[INDEX : INDEX + 1, :], b[INDEX : INDEX + 1, :])
        for a, b in zip(pieces[::2], pieces[1::2])
    ]
    index = jnp.concatenate([i - consts[SHIFT, :] for i in index], axis=1)
    index = jnp.where(index < 0, index + ROWB_DEV, index)
    prods = jnp.concatenate([piece[:NB_DEV, :] for piece in pieces], axis=0)
    front = place_sum(index, prods, ROWS_HELD)
    u = front / alpha - u_raw_before[...] * (alpha / beta[:1, :])
    square = total(u * u)
    if last:
        square_out[...] = jnp.broadcast_to(square, (8, BLK))
        return
    u_raw[...] = u
    times_tiles(tiles, 0, pick(ats[:NB_DEV, :], u), msg)
    write_end(msg, consts[COL_ROW, :], square)


def before_end_kernel(*refs):
    v_raws, alphas, betas = refs[:ITERS], refs[ITERS : 2 * ITERS], refs[2 * ITERS : 3 * ITERS]
    x_out, w_out, scalars = refs[3 * ITERS :]
    alpha = [a[:1, :] for a in alphas]
    beta = [b[:1, :] for b in betas]
    phibar, rhobar = beta[0], alpha[0]
    x = jnp.zeros(x_out.shape, f32)
    w = v_raws[0][...] / alpha[0]
    for k in range(1, ITERS):
        rho = jnp.sqrt(rhobar * rhobar + beta[k] * beta[k])
        cosine, sine = rhobar / rho, beta[k] / rho
        phi = cosine * phibar
        phibar = sine * phibar
        x = x + phi / rho * w
        w = v_raws[k][...] / alpha[k] - sine * alpha[k] / rho * w
        rhobar = -cosine * alpha[k]
    x_out[...] = x
    w_out[...] = w
    row = lax.broadcasted_iota(jnp.int32, (8, BLK), 0)
    scalars[...] = jnp.where(row == 0, phibar, jnp.where(row == 1, rhobar, beta[0]))


def end_kernel(half, other, x, w, scalars, out, residual):
    beta = jnp.sqrt(half[:1, :] + other[:1, :])
    phibar, rhobar, beta_first = scalars[:1, :], scalars[1:2, :], scalars[2:3, :]
    rho = jnp.sqrt(rhobar * rhobar + beta * beta)
    out[...] = x[...] + rhobar / rho * phibar / rho * w[...]
    residual[...] = (beta / rho * phibar / beta_first)[:, :1]


def split_tiles(blocks, blk_row, blk_col, rhs, place):
    rows = blocks.shape[0]
    vmem = pl.BlockSpec(memory_space=pltpu.VMEM)
    there = [pltpu.with_memory_space_constraint(x, pltpu.HBM) for x in (blocks, blk_row, blk_col, rhs)]
    return pl.pallas_call(
        tiles_kernel,
        out_shape=[
            pltpu.VMEM((2 * rows, 2 * BLK), bf16),
            jax.ShapeDtypeStruct((8, BLK), f32),
            jax.ShapeDtypeStruct((2 * NB_DEV, BLK), f32),
            jax.ShapeDtypeStruct(rhs.shape, f32),
        ],
        in_specs=[pl.BlockSpec(memory_space=pl.ANY)] * 4 + [vmem],
        out_specs=[vmem] * 4,
        scratch_shapes=[
            pltpu.VMEM((rows, BLK), f32),
            pltpu.VMEM((1, NB_DEV), jnp.int32),
            pltpu.VMEM((1, NB_DEV), jnp.int32),
            pltpu.SemaphoreType.DMA((PARTS + 3,)),
        ],
        compiler_params=pltpu.CompilerParams(vmem_limit_bytes=VMEM_LIMIT),
        cost_estimate=pl.CostEstimate(flops=0, bytes_accessed=4 * rows * BLK, transcendentals=0),
    )(*there, place)


def call(body, tiles, ins, outs):
    if tiles is not None:
        ins = [pltpu.with_memory_space_constraint(tiles, pltpu.VMEM)] + ins
    return pl.pallas_call(
        body,
        out_shape=[jax.ShapeDtypeStruct(s, f32) for s in outs],
        in_specs=[pl.BlockSpec(memory_space=pltpu.VMEM)] * len(ins),
        out_specs=[pl.BlockSpec(memory_space=pltpu.VMEM)] * len(outs),
        compiler_params=pltpu.CompilerParams(vmem_limit_bytes=VMEM_LIMIT),
    )(*ins)


def chip_steps(chips):
    if chips == 8:
        gathers = [(2, [(3, 4), (1, 5), (6, 7)])] * (ITERS - 1) + [(2, [(1, 7), (3, 5), (6, 4)])]
        return gathers, (1, [(2, 4), (3, 5), (6, 7)])
    steps = 1, [(m, m + 1) for m in range(2, chips, 2)]
    return [steps] * ITERS, steps


def on_device(n_row, n_col, rhs, blocks, blk_row, blk_col):
    chips = n_row // 2
    all_gather_steps, sum_steps = chip_steps(chips)
    per_rhs = rhs.shape[0] // BLK
    per_out = COLB_DEV // n_row
    row, col = lax.axis_index("row"), lax.axis_index("col")

    def swap(x):
        return lax.ppermute(x, "row", [(r, r ^ 1) for r in range(n_row)])

    def to_near(x, steps):
        return lax.ppermute(x, "row", [(r, r ^ (2 * steps[0])) for r in range(n_row)])

    def to_chips(x, steps):
        return [lax.ppermute(x, "row", [(r, r ^ (2 * step[r % 2])) for r in range(n_row)]) for step in steps[1]]

    def around_col(x):
        return [x] + [
            lax.ppermute(x, "col", [(i, (i - s) % n_col) for i in range(n_col)]) for s in range(1, n_col)
        ]

    rhs = rhs.reshape(per_rhs, BLK)
    pieces = around_col(rhs)
    place = jnp.full((8, BLK), col * per_rhs).astype(f32)
    tiles, consts, ats, pieces[0] = split_tiles(
        blocks.reshape(NB_DEV * BLK, BLK), blk_row.reshape(1, NB_DEV), blk_col.reshape(1, NB_DEV), rhs, place
    )
    lane = lax.broadcasted_iota(jnp.int32, (MSG - NB_DEV, BLK), 1)
    end_row = lax.broadcasted_iota(jnp.int32, (MSG - NB_DEV, BLK), 0)

    def gather(msg, gather_steps):
        peer, beside = swap(msg), to_near(jnp.pad(msg, ((0, MSG), (0, 0))), gather_steps)
        a, b = msg[NB_DEV:], peer[NB_DEV:]
        end = jnp.where(end_row == 0, jnp.where(lane < NB_DEV, a, b), a + b)
        both = jnp.concatenate([msg[:NB_DEV], peer[:NB_DEV], end])
        chips = to_chips(both, gather_steps)
        chips = [(c, swap(c)) for c in chips]
        late, soon = sum(chips[:1], ()), sum(chips[1:], ())
        (early,) = call(
            functools.partial(early_kernel, 4), None, [msg, peer, beside, swap(beside), *soon], [(COLB_DEV + 8, BLK)]
        )
        return [early, *late]

    u_raw, msg = call(
        functools.partial(first_kernel, n_col),
        tiles,
        pieces + [consts, ats],
        [(ROWS_HELD, BLK), (MSG, BLK)],
    )
    alphas, betas, v_raws = [], [], []
    for step in range(ITERS):
        msgs = gather(msg, all_gather_steps[step])
        before = [v_raws[-1], alphas[-1]] if step else []
        v_raw, msg, beta = call(
            functools.partial(v_kernel, step > 0, len(msgs)),
            tiles,
            msgs + before + [consts, ats],
            [(COLB_DEV, BLK), (MSG, BLK), (8, BLK)],
        )
        v_raws.append(v_raw)
        betas.append(beta)
        last = step + 1 == ITERS
        ins = [consts, u_raw, beta] + around_col(msg)
        body = functools.partial(u_kernel, n_col, last)
        if last:
            square, alpha = call(body, None, ins, [(8, BLK), (8, BLK)])
        else:
            u_raw, msg, alpha = call(
                body, tiles, ins + [ats], [(ROWS_HELD, BLK), (MSG, BLK), (8, BLK)]
            )
        alphas.append(alpha)

    mine = [lax.dynamic_slice_in_dim(v, row * per_out, per_out) for v in v_raws]
    held = call(before_end_kernel, None, mine + alphas + betas, [(per_out, BLK), (per_out, BLK), (8, BLK)])
    beside = to_near(square, sum_steps)
    half = functools.reduce(lambda a, b: a + b, to_chips(square + swap(square), sum_steps), square + beside)
    out, residual = call(end_kernel, None, [half, swap(half), *held], [(per_out, BLK), (1, 1)])
    return out.reshape(per_out * BLK), residual.reshape(())


def solution(mesh):
    return jax.shard_map(
        functools.partial(on_device, mesh.shape["row"], mesh.shape["col"]),
        mesh=mesh,
        in_specs=(
            P(("row", "col")),
            P("row", "col", None, None, None),
            P("row", "col", None),
            P("row", "col", None),
        ),
        out_specs=(P(("col", "row")), P()),
        check_vma=False,
    )
```

```python
import functools

import jax
import jax.numpy as jnp
from jax import lax
from jax.experimental import pallas as pl
from jax.experimental.pallas import tpu as pltpu
from jax.sharding import PartitionSpec as P

BLK = 128
ROWB_DEV = 496
COLB_DEV = 512
NB_DEV = 64
ITERS = 3
MSG = NB_DEV + 8
INDEX, SQUARE = NB_DEV, NB_DEV + 1
COL_ROW, ROW_ROW, SHIFT = (slice(k, k + 1) for k in range(3))
ROWS_HELD = 512
PARTS = 8
VMEM_LIMIT = 16 * 1024 * 1024

f32 = jnp.float32
bf16 = jnp.bfloat16


def total(x):
    s = jnp.sum(jnp.sum(x, axis=0, keepdims=True), axis=1, keepdims=True)
    return jnp.broadcast_to(s, (1, BLK))


def halves(x):
    high = x.astype(bf16)
    return high, (x - high.astype(f32)).astype(bf16)


def place_sum(index_row, parts, rows):
    k = parts.shape[0]
    at = lax.broadcasted_iota(jnp.int32, (rows, k), 0).astype(f32)
    hot = jnp.where(at == index_row, 1.0, 0.0).astype(bf16)
    out = jnp.dot(hot, jnp.concatenate(halves(parts), axis=1), preferred_element_type=f32)
    return out[:, :BLK] + out[:, BLK:]


def pick(at, x):
    rows = x.shape[0]
    lane = lax.broadcasted_iota(jnp.int32, (NB_DEV, rows), 1).astype(f32)
    hot = jnp.where(lane == jnp.concatenate([at] * (rows // BLK), axis=1), 1.0, 0.0).astype(bf16)
    return jnp.dot(hot, jnp.concatenate(halves(x), axis=1), preferred_element_type=f32)


def times_tiles(tiles, first, picked, msg):
    per = 8
    row = lax.broadcasted_iota(jnp.int32, (2 * per, BLK), 0)
    for g in range(0, NB_DEV, per):
        both = jnp.concatenate([picked[g : g + per, :BLK], picked[g : g + per, BLK:]], axis=0)
        lhs = jnp.concatenate([jnp.where(row % per == t, both, 0.0) for t in range(per)], axis=1).astype(bf16)
        out = jnp.dot(lhs, tiles[(first + g) * BLK : (first + g + per) * BLK, :], preferred_element_type=f32)
        out = out[:, :BLK] + out[:, BLK:]
        msg[g : g + per, :] = out[:per] + out[per:]


def write_end(msg, index_row, square):
    row = lax.broadcasted_iota(jnp.int32, (MSG - NB_DEV, BLK), 0)
    msg[NB_DEV:, :] = jnp.where(row == 0, index_row, jnp.where(row == 1, square, 0.0))


def tiles_kernel(blocks, blk_row, blk_col, rhs, place, out, consts, ats, mine, held, rows_held, cols_held, sems):
    per = held.shape[0] // PARTS
    few = [
        pltpu.make_async_copy(a, b, sems.at[PARTS + k])
        for k, (a, b) in enumerate(((blk_row, rows_held), (blk_col, cols_held), (rhs, mine)))
    ]
    parts = [
        pltpu.make_async_copy(blocks.at[pl.ds(k * per, per)], held.at[pl.ds(k * per, per)], sems.at[k])
        for k in range(PARTS)
    ]
    for part in few + parts:
        part.start()
    for part in few:
        part.wait()
    rows, cols = rows_held[...].astype(f32), cols_held[...].astype(f32)
    shift = place[:1, :]
    consts[COL_ROW, :] = jnp.concatenate([cols, cols], axis=1)
    consts[ROW_ROW, :] = jnp.concatenate([rows, rows], axis=1)
    consts[SHIFT, :] = shift
    consts[3:, :] = jnp.zeros((5, BLK), f32)
    turned = rows - shift[:, :NB_DEV]
    turned = jnp.where(turned < 0, turned + ROWB_DEV, turned)
    ats[...] = jnp.broadcast_to(jnp.concatenate([turned, cols], axis=1), (2 * NB_DEV, BLK)).T
    for k, part in enumerate(parts):
        part.wait()
        for at in range(k * per, (k + 1) * per, BLK):
            for lane, half in zip((0, BLK), halves(held[at : at + BLK, :])):
                out[at : at + BLK, lane : lane + BLK] = half
                out[held.shape[0] + at : held.shape[0] + at + BLK, lane : lane + BLK] = half.T


def first_kernel(n_col, tiles, *refs):
    pieces, (consts, ats, u_raw, msg) = refs[:n_col], refs[n_col:]
    per = pieces[0].shape[0]
    for k, piece in enumerate(pieces):
        u_raw[k * per : (k + 1) * per, :] = piece[...]
    u_raw[ROWB_DEV:, :] = jnp.zeros((ROWS_HELD - ROWB_DEV, BLK), f32)
    u = u_raw[...]
    times_tiles(tiles, 0, pick(ats[:NB_DEV, :], u), msg)
    write_end(msg, consts[COL_ROW, :], total(u * u))


def sum_messages(cores, chips):
    lane = lax.broadcasted_iota(jnp.int32, (1, BLK), 1)
    n = 2 * NB_DEV
    parts, index, square = [], [], jnp.zeros((1, BLK), f32)
    for a, b in zip(cores[::2], cores[1::2]):
        parts += [a[:NB_DEV], b[:NB_DEV]]
        index.append(jnp.where(lane < NB_DEV, a[INDEX : INDEX + 1], b[INDEX : INDEX + 1]))
        square = square + (a[SQUARE : SQUARE + 1] + b[SQUARE : SQUARE + 1])
    for chip in chips:
        parts.append(chip[:n])
        index.append(chip[n : n + 1])
        square = square + chip[n + 1 : n + 2]
    return place_sum(jnp.concatenate(index, axis=1), jnp.concatenate(parts, axis=0), COLB_DEV), square


def early_kernel(n_cores, *refs):
    *msgs, out = refs
    back, square = sum_messages(msgs[:n_cores], msgs[n_cores:])
    out[:COLB_DEV, :] = back
    out[COLB_DEV:, :] = jnp.broadcast_to(square, (8, BLK))


def v_kernel(has_before, n_msgs, tiles, *refs):
    msgs, refs = refs[:n_msgs], refs[n_msgs:]
    if has_before:
        v_raw_before, alpha, consts, ats, v_raw, msg, beta_out = refs
    else:
        consts, ats, v_raw, msg, beta_out = refs
    early, *chips = msgs
    back, square = sum_messages([], chips)
    beta = jnp.sqrt(early[COLB_DEV : COLB_DEV + 1, :] + square)
    v = (early[:COLB_DEV, :] + back) / beta
    if has_before:
        v = v - v_raw_before[...] * (beta / alpha[:1, :])
    v_raw[...] = v
    beta_out[...] = jnp.broadcast_to(beta, (8, BLK))
    times_tiles(tiles, NB_DEV, pick(ats[NB_DEV:, :], v), msg)
    write_end(msg, consts[ROW_ROW, :], total(v * v))


def u_kernel(n_col, last, *refs):
    if not last:
        tiles, *refs = refs
    consts, u_raw_before, beta, *refs = refs
    pieces, refs = refs[:n_col], refs[n_col:]
    if last:
        square_out, alpha_out = refs
    else:
        ats, u_raw, msg, alpha_out = refs
    square = pieces[0][SQUARE : SQUARE + 1, :]
    for piece in pieces[1:]:
        square = square + piece[SQUARE : SQUARE + 1, :]
    alpha = jnp.sqrt(square)
    alpha_out[...] = jnp.broadcast_to(alpha, (8, BLK))
    lane = lax.broadcasted_iota(jnp.int32, (1, BLK), 1)
    index = [
        jnp.where(lane < NB_DEV, a[INDEX : INDEX + 1, :], b[INDEX : INDEX + 1, :])
        for a, b in zip(pieces[::2], pieces[1::2])
    ]
    index = jnp.concatenate([i - consts[SHIFT, :] for i in index], axis=1)
    index = jnp.where(index < 0, index + ROWB_DEV, index)
    prods = jnp.concatenate([piece[:NB_DEV, :] for piece in pieces], axis=0)
    front = place_sum(index, prods, ROWS_HELD)
    u = front / alpha - u_raw_before[...] * (alpha / beta[:1, :])
    square = total(u * u)
    if last:
        square_out[...] = jnp.broadcast_to(square, (8, BLK))
        return
    u_raw[...] = u
    times_tiles(tiles, 0, pick(ats[:NB_DEV, :], u), msg)
    write_end(msg, consts[COL_ROW, :], square)


def before_end_kernel(*refs):
    v_raws, alphas, betas = refs[:ITERS], refs[ITERS : 2 * ITERS], refs[2 * ITERS : 3 * ITERS]
    x_out, w_out, scalars = refs[3 * ITERS :]
    alpha = [a[:1, :] for a in alphas]
    beta = [b[:1, :] for b in betas]
    phibar, rhobar = beta[0], alpha[0]
    x = jnp.zeros(x_out.shape, f32)
    w = v_raws[0][...] / alpha[0]
    for k in range(1, ITERS):
        rho = jnp.sqrt(rhobar * rhobar + beta[k] * beta[k])
        cosine, sine = rhobar / rho, beta[k] / rho
        phi = cosine * phibar
        phibar = sine * phibar
        x = x + phi / rho * w
        w = v_raws[k][...] / alpha[k] - sine * alpha[k] / rho * w
        rhobar = -cosine * alpha[k]
    x_out[...] = x
    w_out[...] = w
    row = lax.broadcasted_iota(jnp.int32, (8, BLK), 0)
    scalars[...] = jnp.where(row == 0, phibar, jnp.where(row == 1, rhobar, beta[0]))


def end_kernel(half, other, x, w, scalars, out, residual):
    beta = jnp.sqrt(half[:1, :] + other[:1, :])
    phibar, rhobar, beta_first = scalars[:1, :], scalars[1:2, :], scalars[2:3, :]
    rho = jnp.sqrt(rhobar * rhobar + beta * beta)
    out[...] = x[...] + rhobar / rho * phibar / rho * w[...]
    residual[...] = (beta / rho * phibar / beta_first)[:, :1]


def split_tiles(blocks, blk_row, blk_col, rhs, place):
    rows = blocks.shape[0]
    vmem = pl.BlockSpec(memory_space=pltpu.VMEM)
    there = [pltpu.with_memory_space_constraint(x, pltpu.HBM) for x in (blocks, blk_row, blk_col, rhs)]
    return pl.pallas_call(
        tiles_kernel,
        out_shape=[
            pltpu.VMEM((2 * rows, 2 * BLK), bf16),
            jax.ShapeDtypeStruct((8, BLK), f32),
            jax.ShapeDtypeStruct((2 * NB_DEV, BLK), f32),
            jax.ShapeDtypeStruct(rhs.shape, f32),
        ],
        in_specs=[pl.BlockSpec(memory_space=pl.ANY)] * 4 + [vmem],
        out_specs=[vmem] * 4,
        scratch_shapes=[
            pltpu.VMEM((rows, BLK), f32),
            pltpu.VMEM((1, NB_DEV), jnp.int32),
            pltpu.VMEM((1, NB_DEV), jnp.int32),
            pltpu.SemaphoreType.DMA((PARTS + 3,)),
        ],
        compiler_params=pltpu.CompilerParams(vmem_limit_bytes=VMEM_LIMIT),
        cost_estimate=pl.CostEstimate(flops=0, bytes_accessed=4 * rows * BLK, transcendentals=0),
    )(*there, place)


def call(body, tiles, ins, outs):
    if tiles is not None:
        ins = [pltpu.with_memory_space_constraint(tiles, pltpu.VMEM)] + ins
    return pl.pallas_call(
        body,
        out_shape=[jax.ShapeDtypeStruct(s, f32) for s in outs],
        in_specs=[pl.BlockSpec(memory_space=pltpu.VMEM)] * len(ins),
        out_specs=[pl.BlockSpec(memory_space=pltpu.VMEM)] * len(outs),
        compiler_params=pltpu.CompilerParams(vmem_limit_bytes=VMEM_LIMIT),
    )(*ins)


def chip_steps(chips):
    if chips == 8:
        return (2, [(1, 4), (3, 5), (6, 7)]), (1, [(2, 4), (3, 5), (6, 7)])
    steps = 1, [(m, m + 1) for m in range(2, chips, 2)]
    return steps, steps


def on_device(n_row, n_col, rhs, blocks, blk_row, blk_col):
    chips = n_row // 2
    gather_steps, sum_steps = chip_steps(chips)
    per_rhs = rhs.shape[0] // BLK
    per_out = COLB_DEV // n_row
    row, col = lax.axis_index("row"), lax.axis_index("col")

    def swap(x):
        return lax.ppermute(x, "row", [(r, r ^ 1) for r in range(n_row)])

    def to_near(x, steps):
        return lax.ppermute(x, "row", [(r, r ^ (2 * steps[0])) for r in range(n_row)])

    def to_chips(x, steps):
        return [lax.ppermute(x, "row", [(r, r ^ (2 * step[r % 2])) for r in range(n_row)]) for step in steps[1]]

    def around_col(x):
        return [x] + [
            lax.ppermute(x, "col", [(i, (i - s) % n_col) for i in range(n_col)]) for s in range(1, n_col)
        ]

    rhs = rhs.reshape(per_rhs, BLK)
    pieces = around_col(rhs)
    place = jnp.full((8, BLK), col * per_rhs).astype(f32)
    tiles, consts, ats, pieces[0] = split_tiles(
        blocks.reshape(NB_DEV * BLK, BLK), blk_row.reshape(1, NB_DEV), blk_col.reshape(1, NB_DEV), rhs, place
    )
    lane = lax.broadcasted_iota(jnp.int32, (MSG - NB_DEV, BLK), 1)
    end_row = lax.broadcasted_iota(jnp.int32, (MSG - NB_DEV, BLK), 0)

    def gather(msg):
        peer, beside = swap(msg), to_near(jnp.pad(msg, ((0, MSG), (0, 0))), gather_steps)
        a, b = msg[NB_DEV:], peer[NB_DEV:]
        end = jnp.where(end_row == 0, jnp.where(lane < NB_DEV, a, b), a + b)
        both = jnp.concatenate([msg[:NB_DEV], peer[:NB_DEV], end])
        chips = to_chips(both, gather_steps)
        chips = [(c, swap(c)) for c in chips]
        late, soon = sum(chips[:1], ()), sum(chips[1:], ())
        (early,) = call(
            functools.partial(early_kernel, 4), None, [msg, peer, beside, swap(beside), *soon], [(COLB_DEV + 8, BLK)]
        )
        return [early, *late]

    u_raw, msg = call(
        functools.partial(first_kernel, n_col),
        tiles,
        pieces + [consts, ats],
        [(ROWS_HELD, BLK), (MSG, BLK)],
    )
    alphas, betas, v_raws = [], [], []
    for step in range(ITERS):
        msgs = gather(msg)
        before = [v_raws[-1], alphas[-1]] if step else []
        v_raw, msg, beta = call(
            functools.partial(v_kernel, step > 0, len(msgs)),
            tiles,
            msgs + before + [consts, ats],
            [(COLB_DEV, BLK), (MSG, BLK), (8, BLK)],
        )
        v_raws.append(v_raw)
        betas.append(beta)
        last = step + 1 == ITERS
        ins = [consts, u_raw, beta] + around_col(msg)
        body = functools.partial(u_kernel, n_col, last)
        if last:
            square, alpha = call(body, None, ins, [(8, BLK), (8, BLK)])
        else:
            u_raw, msg, alpha = call(
                body, tiles, ins + [ats], [(ROWS_HELD, BLK), (MSG, BLK), (8, BLK)]
            )
        alphas.append(alpha)

    mine = [lax.dynamic_slice_in_dim(v, row * per_out, per_out) for v in v_raws]
    held = call(before_end_kernel, None, mine + alphas + betas, [(per_out, BLK), (per_out, BLK), (8, BLK)])
    beside = to_near(square, sum_steps)
    half = functools.reduce(lambda a, b: a + b, to_chips(square + swap(square), sum_steps), square + beside)
    out, residual = call(end_kernel, None, [half, swap(half), *held], [(per_out, BLK), (1, 1)])
    return out.reshape(per_out * BLK), residual.reshape(())


def solution(mesh):
    return jax.shard_map(
        functools.partial(on_device, mesh.shape["row"], mesh.shape["col"]),
        mesh=mesh,
        in_specs=(
            P(("row", "col")),
            P("row", "col", None, None, None),
            P("row", "col", None),
            P("row", "col", None),
        ),
        out_specs=(P(("col", "row")), P()),
        check_vma=False,
    )
```
